256 devices in a mesh: layer: 8 (over y, core), row: 32 (over z, x).
Axes of the slice: x: 4, y: 4, z: 8, core: 2. Of those that a mesh axis runs over, the one named last changes fastest.
Arguments:
- hidden_stack: bfloat16 [8, 3, 256, 28672], P('layer', None, 'row'), may hold values from -1.296875 to 1.296875
- model_stack: bfloat16 [8, 3, 256, 8192], P('layer', None, 'row'), may hold values from -1.296875 to 1.296875
- tenant_weights: float32 [8], replicated, may hold values from 0.5 to 2
- ranks: int32 [8], replicated, may hold values from 8 to 64, as said below
- start_basis: float32 [8, 256, 128], P('layer'), may hold values from -6 to 6
Outputs:
- serving_tiles: bfloat16 [8, 3, 2048, 8192], P(None, None, 'row', 'layer')
The draws below stay inside these ranges and needn't reach their ends.
Inputs may be any that keep to these rules, and one draw needn't show every extreme that they name: The 8 ranks sum to 256; both the least and the most are taken by some tenant.
All inputs are finite; a program needn't handle non-finite values.
Results may differ from the reference program's by a relative error of at most 0.0057.
Values may be sent and summed in bfloat16 or wider, within the bound.
A program may use at most 128 MiB of HBM per device.

```python
import math
import jax
import jax.numpy as jnp
from jax import lax

D = 8192
FF = 28672
RANK_SUM = 256
TENANTS = 8
KEEP = 128
ITERS = 3
SERVE_DEV = 64
MOST_RANK = 64
LEAST_RANK = 8
LAYERS = 8
SERVE_ROWS = 2048
N_ROW = 32


def draw_ranks(key, part):
    key = jax.random.fold_in(key, 7)
    first_key, second_key, order_key = jax.random.split(key, 3)
    paired = jax.random.randint(first_key, (2,), LEAST_RANK, MOST_RANK - LEAST_RANK + 1)
    single = jax.random.randint(second_key, (1,), LEAST_RANK, MOST_RANK - 2 * LEAST_RANK + 1)
    fixed_pair = jnp.array([MOST_RANK, LEAST_RANK], dtype=jnp.int32)
    values = jnp.concatenate([fixed_pair, paired, MOST_RANK - paired, single, MOST_RANK - LEAST_RANK - single])
    order = jax.random.permutation(order_key, 8)
    return values[order].astype(jnp.int32)


def levels(own_key, extent, pieces, low, top_value):
    def one(position, blocks):
        heights = jax.random.uniform(jax.random.fold_in(jax.random.fold_in(own_key, 6), position), (blocks,), jnp.float32, low / len(pieces), top_value / len(pieces))
        return jnp.repeat(jnp.exp(heights), extent[position] // blocks).reshape((-1,) + (1,) * (len(extent) - position - 1))

    loudness = one(*pieces[0])
    for cut in pieces[1:]:
        loudness = loudness * one(*cut)
    return loudness


def normal_values(key, dims, deviation, reach, cuts=(), kind=jnp.bfloat16):
    values = jax.random.normal(key, dims, jnp.float32) * deviation
    if len(cuts) > 0:
        values = levels(key, dims, cuts, -0.22, 0.18) * values
    return jnp.clip(values, min=-reach, max=reach).astype(kind)


def setup_inputs(seed: int = 0) -> dict:
    key_list = jax.random.split(jax.random.key(seed), 6)
    return {
        "hidden_stack": normal_values(key_list[0], (LAYERS, 3, RANK_SUM, FF), 0.21, 1.296875, ((0, 8), (2, 32))),
        "model_stack": normal_values(key_list[1], (LAYERS, 3, RANK_SUM, D), 0.21, 1.296875, ((0, 8), (2, 32))),
        "tenant_weights": jnp.clip(jnp.exp(jax.random.uniform(key_list[2], (TENANTS,), jnp.float32, math.log(0.5), math.log(2.0))), 0.5, 2.0),
        "ranks": draw_ranks(jax.random.fold_in(key_list[5], 71), 0),
        "start_basis": normal_values(key_list[4], (LAYERS, RANK_SUM, KEEP), 1.0, 6.0, ((0, 8),), jnp.float32),
    }


def column_scale(ranks, tenant_weights, width):
    ends = jnp.cumsum(ranks).astype(jnp.int32)
    begins = (ends - ranks).astype(jnp.int32)
    columns = jnp.arange(width, dtype=jnp.int32)[:, None]
    owner = ((columns >= begins[None, :]) & (columns < ends[None, :])).astype(jnp.float32)
    factor = tenant_weights.astype(jnp.float32) * jnp.sqrt(MOST_RANK / ranks.astype(jnp.float32))
    return jnp.dot(owner, factor, precision=lax.Precision.HIGHEST)

def cholesky_pass(matrix):
    product = jnp.dot(matrix.T, matrix, precision=lax.Precision.HIGHEST)
    factor = jnp.linalg.cholesky(product)
    return jax.scipy.linalg.solve_triangular(factor, matrix.T, lower=True).T

def orthonormal(matrix):
    return cholesky_pass(cholesky_pass(matrix))

def one_layer(stacks, scale):
    hidden_layer, model_layer, start_layer = stacks
    outer = scale[:, None] * scale[None, :]
    tiles = []
    for proj in range(3):
        hidden_part = hidden_layer[proj]
        model_part = model_layer[proj]
        gram_hidden = jnp.dot(hidden_part.astype(jnp.float32), hidden_part.T.astype(jnp.float32), preferred_element_type=jnp.float32)
        gram_model = jnp.dot(model_part.astype(jnp.float32), model_part.T.astype(jnp.float32), preferred_element_type=jnp.float32) * outer
        lower = jnp.linalg.cholesky(gram_model)
        basis = start_layer
        for sweep in range(ITERS):
            lifted = jnp.dot(lower, basis, precision=lax.Precision.HIGHEST)
            pushed = jnp.dot(gram_hidden, lifted, precision=lax.Precision.HIGHEST)
            basis = orthonormal(jnp.dot(lower.T, pushed, precision=lax.Precision.HIGHEST))
        lifted = jnp.dot(lower, basis, precision=lax.Precision.HIGHEST)
        pulled = scale[:, None] * jax.scipy.linalg.solve_triangular(lower, basis, lower=True, trans=1)
        window = hidden_part.reshape(RANK_SUM, N_ROW, FF // N_ROW)[:, :, :SERVE_DEV].reshape(RANK_SUM, SERVE_ROWS)
        left = jnp.dot(window.astype(jnp.float32).T, lifted, precision=lax.Precision.HIGHEST).astype(jnp.bfloat16)
        right = jnp.dot(model_part.astype(jnp.float32).T, pulled, precision=lax.Precision.HIGHEST).astype(jnp.bfloat16)
        tiles.append(jnp.dot(left.astype(jnp.float32), right.T.astype(jnp.float32), preferred_element_type=jnp.float32).astype(jnp.bfloat16))
    return jnp.stack(tiles)

def reference(hidden_stack, model_stack, tenant_weights, ranks, start_basis):
    scale = column_scale(ranks, tenant_weights, RANK_SUM)
    return lax.map(lambda stacks: one_layer(stacks, scale), (hidden_stack, model_stack, start_basis))
```

```python
import functools
import jax
import jax.numpy as jnp
from jax import lax
from jax.experimental import pallas as pl
from jax.experimental.pallas import tpu as pltpu
from jax.sharding import PartitionSpec as P

ITERS = 3
SERVE_DEV = 64
MOST_RANK = 64
PROJ = 3
HI = lax.Precision.HIGHEST
MESH = pl.DeviceIdType.MESH
VM = pl.BlockSpec(memory_space=pltpu.VMEM)
ANY = pl.BlockSpec(memory_space=pl.ANY)
SM = pl.BlockSpec(memory_space=pltpu.SMEM)
VMEM_BYTES = 48 * 1024 * 1024


def dot_hi(a, b, dims):
    return lax.dot_general(a, b, (dims, ((), ())), precision=HI, preferred_element_type=jnp.float32)


def spread_lane(tile, lane):
    return jnp.broadcast_to(tile[:, lane:lane + 1], (8, 128))


def spread_row(tile, row):
    return jnp.broadcast_to(tile[row:row + 1, :], (8, 128))


def factor(matrix, need_upper, need_inverse):
    sub = lax.broadcasted_iota(jnp.int32, (8, 128), 0)
    lane = lax.broadcasted_iota(jnp.int32, (8, 128), 1)
    rows = [matrix[8 * k:8 * k + 8, :] for k in range(16)]
    inverse = [jnp.where(lane == sub + 8 * k, 1.0, 0.0).astype(jnp.float32) for k in range(16)]
    upper_rows, inverse_rows = [], []
    for k in range(16):
        panel, ipanel = rows[k], inverse[k]
        cols = [spread_lane(panel, 8 * k + c) for c in range(8)]
        raw, iraw, diag = panel, ipanel, panel
        for j in range(8):
            pivot = spread_row(cols[j], j)
            recip = 1.0 / pivot
            scaled = cols[j] * recip
            here = sub == j
            prow = spread_row(panel, j)
            irow = spread_row(ipanel, j)
            raw = jnp.where(here, prow, raw)
            iraw = jnp.where(here, irow, iraw)
            diag = jnp.where(here, pivot, diag)
            panel = jnp.where(here, prow * recip, panel - scaled * prow)
            if need_inverse:
                ipanel = jnp.where(here, irow * recip, ipanel - scaled * irow)
            for c in range(j + 1, 8):
                crow = spread_row(cols[c], j)
                cols[c] = jnp.where(here, crow * recip, cols[c] - scaled * crow)
        root = lax.rsqrt(diag)
        upper_rows.append(raw * root)
        inverse_rows.append(iraw * root)
        prows = [spread_row(panel, c) for c in range(8)]
        irows = [spread_row(ipanel, c) for c in range(8)]
        for i in range(k + 1, 16):
            coef = [spread_lane(rows[i], 8 * k + c) for c in range(8)]
            rows[i] = rows[i] - sum(coef[c] * prows[c] for c in range(8))
            if need_inverse:
                inverse[i] = inverse[i] - sum(coef[c] * irows[c] for c in range(8))
    out = []
    if need_upper:
        rowi = lax.broadcasted_iota(jnp.int32, (128, 128), 0)
        coli = lax.broadcasted_iota(jnp.int32, (128, 128), 1)
        up = jnp.concatenate(upper_rows, axis=0)
        out.append(jnp.where(coli >= rowi, up, 0.0))
    if need_inverse:
        out.append(jnp.concatenate(inverse_rows, axis=0))
    return out


def place():
    layer = lax.axis_index("layer")
    row = lax.axis_index("row")
    return layer, row, row // 4, row % 4


def remote(src, dst, send, recv, layer, row):
    return pltpu.make_async_remote_copy(
        src_ref=src, dst_ref=dst, send_sem=send, recv_sem=recv,
        device_id=(layer, row), device_id_type=MESH,
    )


def wait_bytes(ref, sem):
    pltpu.make_async_copy(ref, ref, sem).wait()


def pack_gram(buf, part):
    ranks = buf.shape[0] * buf.shape[1]
    factors = buf[...].astype(jnp.float32).reshape(ranks, buf.shape[2]).astype(jnp.bfloat16)
    gram = lax.dot_general(
        factors, factors, (((1,), (1,)), ((), ())), preferred_element_type=jnp.float32
    )
    part[:, :, 0:128] = gram[0:128, 0:128].reshape(8, 16, 128)
    part[:, :, 128:384] = gram[128:256, :].reshape(8, 16, 256)


def start_reduce(part, slots, send, recv, layer, z, x):
    def one(k, carry):
        to = (z + k) % 8
        remote(part.at[to], slots.at[z], send, recv, layer, to * 4 + x).start()
        return carry

    lax.fori_loop(1, 8, one, 0)
    slots[pl.ds(z, 1)] = part[pl.ds(z, 1)]


def start_share(slots, out, send, recv, send2, recv2, layer, z, x):
    wait_bytes(slots.at[pl.ds(0, 7)], recv)
    wait_bytes(slots.at[pl.ds(0, 7)], send)
    total = slots[0]
    for k in range(1, 8):
        total = total + slots[k]
    out[pl.ds(z, 1)] = total[None]

    def one(k, carry):
        to = (z + k) % 8
        remote(out.at[z], out.at[z], send2, recv2, layer, to * 4 + x).start()
        return carry

    lax.fori_loop(1, 8, one, 0)


def end_share(out, send2, recv2):
    wait_bytes(out.at[pl.ds(0, 7)], recv2)
    wait_bytes(out.at[pl.ds(0, 7)], send2)


def gram_kernel(f_ref, m_ref, gm_ref, gh_ref, mbuf, win, fbuf, part_m, part_h, slots_m, slots_h, sems):
    layer, row, z, x = place()
    barrier = pltpu.get_barrier_semaphore()

    def greet(k, carry):
        pl.semaphore_signal(barrier, inc=1, device_id=(layer, (row + k) % 32), device_id_type=MESH)
        return carry

    lax.fori_loop(1, 32, greet, 0)
    pl.semaphore_wait(barrier, 31)
    mwide, fwide = mbuf.shape[2], fbuf.shape[2]

    def pieces(src_ref, wide, to):
        column = pl.multiple_of((to // 4) * wide, 128)
        return src_ref.at[0, to % 4, :, pl.ds(column, wide)]

    for src_ref, buf, wide, base in ((m_ref, mbuf, mwide, 0), (f_ref, fbuf, fwide, 2)):
        def send(k, carry):
            to = (row + k) % 32

            @pl.when(to % 4 < PROJ)
            def _():
                remote(
                    pieces(src_ref, wide, to), buf.at[row], sems.at[base], sems.at[base + 1], layer, to
                ).start()

            return carry

        lax.fori_loop(1, 32, send, 0)

        @pl.when(x < PROJ)
        def _():
            pltpu.make_async_copy(pieces(src_ref, wide, row), buf.at[row], sems.at[base + 1]).start()

    @pl.when(x < PROJ)
    def _():
        wait_bytes(mbuf, sems.at[1])
        pack_gram(mbuf, part_m)
        start_reduce(part_m, slots_m, sems.at[4], sems.at[5], layer, z, x)
        start_share(slots_m, gm_ref, sems.at[4], sems.at[5], sems.at[6], sems.at[7], layer, z, x)
        wait_bytes(fbuf, sems.at[3])
        pack_gram(fbuf, part_h)
        start_reduce(part_h, slots_h, sems.at[8], sems.at[9], layer, z, x)
        for j in range(4):
            win[:, :, 128 * j:128 * j + 128] = fbuf[:, :, 896 * j:896 * j + 128]
        start_share(slots_h, gh_ref, sems.at[8], sems.at[9], sems.at[10], sems.at[11], layer, z, x)
        end_share(gm_ref, sems.at[6], sems.at[7])
        end_share(gh_ref, sems.at[10], sems.at[11])
        wait_bytes(mbuf.at[pl.ds(0, 23)], sems.at[0])
        wait_bytes(fbuf.at[pl.ds(0, 23)], sems.at[2])

    @pl.when(x >= PROJ)
    def _():
        wait_bytes(mbuf.at[pl.ds(0, 24)], sems.at[0])
        wait_bytes(fbuf.at[pl.ds(0, 24)], sems.at[2])


def column_scale(ranks_ref, weights_ref, index):
    total = jnp.zeros(index.shape, jnp.float32)
    begin = 0
    for t in range(8):
        end = begin + ranks_ref[t]
        rank = jnp.full(index.shape, ranks_ref[t].astype(jnp.float32))
        factor_t = weights_ref[t] * jnp.sqrt(MOST_RANK / rank)
        total = jnp.where((index >= begin) & (index < end), factor_t, total)
        begin = end
    return total


def core_kernel(gm_ref, gh_ref, mbuf, win, weights_ref, ranks_ref, start_ref, left_ref, right_ref,
                lower_s, upper_s, pulled_map, basis_s, both_s):
    row = lax.axis_index("row")

    @pl.when(row % 4 < PROJ)
    def _():
        scale_col = column_scale(ranks_ref, weights_ref, lax.broadcasted_iota(jnp.int32, (256, 1), 0))
        scale_row = column_scale(ranks_ref, weights_ref, lax.broadcasted_iota(jnp.int32, (1, 256), 1))
        packed = gm_ref[...].reshape(128, 384)
        first = packed[:, 0:128] * (scale_col[0:128] * scale_row[:, 0:128])
        cross = packed[:, 128:256] * (scale_col[128:256] * scale_row[:, 0:128])
        last = packed[:, 256:384] * (scale_col[128:256] * scale_row[:, 128:256])
        upper_first, inverse_first = factor(first, True, True)
        low = dot_hi(cross, inverse_first, ((1,), (1,)))
        (upper_last,) = factor(last - dot_hi(low, low, ((1,), (1,))), True, False)
        zero = jnp.zeros((128, 128), jnp.float32)
        upper_s[0:128, 0:128] = upper_first
        upper_s[0:128, 128:256] = low.T
        upper_s[128:256, 0:128] = zero
        upper_s[128:256, 128:256] = upper_last
        lower_s[0:128, 0:128] = upper_first.T
        lower_s[0:128, 128:256] = zero
        lower_s[128:256, 0:128] = low
        lower_s[128:256, 128:256] = upper_last.T
        packed = gh_ref[...].reshape(128, 384)
        hidden = jnp.concatenate(
            [
                jnp.concatenate([packed[:, 0:128], packed[:, 128:256].T], axis=1),
                packed[:, 128:384],
            ],
            axis=0,
        )
        pulled_map[...] = dot_hi(hidden, lower_s[...], ((1,), (0,)))
        basis_s[...] = start_ref[0]

        def sweep(_, carry):
            pushed = dot_hi(pulled_map[...], basis_s[...], ((1,), (0,)))
            both_s[0:256, :] = dot_hi(upper_s[...], pushed, ((1,), (0,)))
            both_s[256:512, :] = pushed

            def one_pass(_, inner):
                raised = both_s[0:256, :]
                (inverse,) = factor(dot_hi(raised, raised, ((0,), (0,))), False, True)
                both_s[...] = dot_hi(both_s[...], inverse, ((1,), (1,)))
                return inner

            lax.fori_loop(0, 2, one_pass, 0)
            basis_s[...] = both_s[0:256, :]
            return carry

        lax.fori_loop(0, ITERS, sweep, 0)
        lifted = dot_hi(lower_s[...], basis_s[...], ((1,), (0,)))
        pulled = scale_col * both_s[256:512, :]
        window = win[...].astype(jnp.float32).reshape(256, 512)
        left = dot_hi(window, lifted, ((0,), (0,)))
        for j in range(4):
            left_ref[j] = left[128 * j:128 * j + SERVE_DEV].astype(jnp.bfloat16)
        model = mbuf[...].astype(jnp.float32).reshape(256, 1024)
        right = dot_hi(pulled, model, ((0,), (0,))).astype(jnp.bfloat16)
        for c in range(8):
            right_ref[c] = right[:, 128 * c:128 * c + 128]


def gather_kernel(left_ref, right_ref, lall, rall, in_send, in_recv, left_send, left_recv,
                  ring_send, ring_recv, side_send, side_recv, wide_send, wide_recv, pass_send, pass_recv):
    layer, row, z, x = place()
    barrier = pltpu.get_barrier_semaphore()

    def greet(to_layer, to_row):
        pl.semaphore_signal(barrier, inc=1, device_id=(to_layer, to_row), device_id_type=MESH)

    def row_at(to_z, to_x):
        return (to_z % 8) * 4 + to_x % 4

    owner = layer == z
    real = x < PROJ
    for k in range(1, 8):
        greet((layer + k) % 8, row)
    for k in range(1, 4):
        greet(layer, row_at(z, x + k))
    greet(layer, row_at(z + 1, x))
    greet(layer, row_at(z + 7, x))
    @pl.when(real & (layer != z))
    def _():
        for l in range(8):
            ring_peer = (layer == (z + 1) % 8) | (layer == (z + 7) % 8)

            @pl.when(jnp.logical_not(ring_peer & (layer == l)))
            def _():
                greet(l, row_at(layer, x))

    pl.semaphore_wait(barrier, 12 + jnp.where(real, 7 - jnp.where(owner, 2, 0), 0))

    @pl.when(real)
    def _():
        for c in range(8):
            mine = rall.at[layer, x, c]

            @pl.when(owner & (z == c))
            def _():
                pltpu.make_async_copy(right_ref.at[c], mine, in_recv.at[0]).start()

            @pl.when(jnp.logical_not(owner & (z == c)))
            def _():
                remote(right_ref.at[c], mine, in_send.at[0], in_recv.at[0], z, row_at(c, x)).start()

        for k in range(1, 4):
            to = (x + k) % 4
            remote(left_ref.at[to], lall.at[layer, x], in_send.at[1], in_recv.at[1],
                   layer, row_at(z, to)).start()
        pltpu.make_async_copy(left_ref.at[x], lall.at[layer, x], in_recv.at[1]).start()

    wait_bytes(lall.at[layer], in_recv.at[1])
    for k in range(1, 8):
        to = (layer + k) % 8
        remote(lall.at[layer], lall.at[layer], left_send, left_recv, to, row).start()

    def shard(low, high, p, c):
        return rall.at[pl.ds(low, high - low), p, c % 8]

    def thick(low, high, c):
        return rall.at[pl.ds(low, high - low), :, c % 8]

    def ring(step, group):
        low = 4 * group
        cut = thick if group else lambda a, b, c: shard(a, b, x, c)
        up_high = low + (4 if step < 3 else 2)
        down_low = low + (0 if step < 3 else 2)
        up = remote(cut(low, up_high, z + 8 - step), cut(low, up_high, z + 8 - step),
                    ring_send.at[group, 0, step], ring_recv.at[group, 0, step], layer, row_at(z + 1, x))
        down = remote(cut(down_low, low + 4, z + step), cut(down_low, low + 4, z + step),
                      ring_send.at[group, 1, step], ring_recv.at[group, 1, step], layer, row_at(z + 7, x))
        return up, down

    def ring_got(step, group):
        low = 4 * group
        cut = thick if group else lambda a, b, c: shard(a, b, x, c)
        up_high = low + (4 if step < 3 else 2)
        down_low = low + (0 if step < 3 else 2)
        wait_bytes(cut(low, up_high, z + 7 - step), ring_recv.at[group, 0, step])
        wait_bytes(cut(down_low, low + 4, z + 1 + step), ring_recv.at[group, 1, step])

    def columns(turn):
        if turn == 0:
            return (z,)
        if turn == 4:
            return (z + 4,)
        return (z + 8 - turn, z + turn)

    def widen(turn):
        for n, c in enumerate(columns(turn)):
            piece = shard(0, 4, x, c)
            remote(piece, piece, wide_send.at[0, turn, n], wide_recv.at[0, turn, n],
                   layer, row_at(z, x + 1)).start()
            remote(piece, piece, wide_send.at[1, turn, n], wide_recv.at[1, turn, n],
                   layer, row_at(z, x + 3)).start()

    def widen_sent(turn):
        for n, c in enumerate(columns(turn)):
            piece = shard(0, 4, x, c)
            wait_bytes(piece, wide_send.at[0, turn, n])
            wait_bytes(piece, wide_send.at[1, turn, n])

    before, after = (x + 3) % 4, (x + 1) % 4

    def relay(turn):
        for n, c in enumerate(columns(turn)):
            @pl.when(before < PROJ)
            def _():
                wait_bytes(shard(0, 4, before, c), wide_recv.at[0, turn, n])
                piece = shard(0, 2, before, c)
                remote(piece, piece, pass_send.at[0, turn, n], pass_recv.at[0, turn, n],
                       layer, row_at(z, x + 1)).start()

            @pl.when(after < PROJ)
            def _():
                wait_bytes(shard(0, 4, after, c), wide_recv.at[1, turn, n])
                piece = shard(2, 4, after, c)
                remote(piece, piece, pass_send.at[1, turn, n], pass_recv.at[1, turn, n],
                       layer, row_at(z, x + 3)).start()

    def relay_end(turn):
        far = (x + 2) % 4
        for n, c in enumerate(columns(turn)):
            @pl.when(before < PROJ)
            def _():
                wait_bytes(shard(0, 2, before, c), pass_send.at[0, turn, n])

            @pl.when(after < PROJ)
            def _():
                wait_bytes(shard(2, 4, after, c), pass_send.at[1, turn, n])

            @pl.when(far < PROJ)
            def _():
                wait_bytes(shard(0, 2, far, c), pass_recv.at[0, turn, n])
                wait_bytes(shard(2, 4, far, c), pass_recv.at[1, turn, n])

    @pl.when(real)
    def _():
        wait_bytes(rall.at[:, x, z], in_recv.at[0])
        piece = shard(4, 8, x, z)
        for k in range(1, 4):
            remote(piece, piece, side_send.at[k - 1], side_recv.at[k - 1], layer, row_at(z, x + k)).start()
        for copy in ring(0, 0):
            copy.start()
        widen(0)

    for k in range(1, 4):
        source = (x + 4 - k) % 4

        @pl.when(source < PROJ)
        def _():
            wait_bytes(shard(4, 8, source, z), side_recv.at[k - 1])

    for copy in ring(0, 1):
        copy.start()
    for step in range(4):
        @pl.when(real)
        def _():
            ring_got(step, 0)
            if step < 3:
                for copy in ring(step + 1, 0):
                    copy.start()
            widen(step + 1)

        ring_got(step, 1)
        if step < 3:
            for copy in ring(step + 1, 1):
                copy.start()
        relay(step)
    relay(4)
    for turn in range(5):
        relay_end(turn)
    for step in range(4):
        for copy in ring(step, 1):
            copy.wait_send()

    @pl.when(real)
    def _():
        for turn in range(5):
            widen_sent(turn)
        for step in range(4):
            for copy in ring(step, 0):
                copy.wait_send()
        piece = shard(4, 8, x, z)
        for k in range(1, 4):
            wait_bytes(piece, side_send.at[k - 1])

        @pl.when(owner)
        def _():
            wait_bytes(right_ref.at[pl.ds(0, 7)], in_send.at[0])

        @pl.when(jnp.logical_not(owner))
        def _():
            wait_bytes(right_ref, in_send.at[0])

        wait_bytes(left_ref.at[pl.ds(0, 3)], in_send.at[1])

    wait_bytes(lall.at[pl.ds(0, 7)], left_send)
    wait_bytes(lall.at[pl.ds(0, 7)], left_recv)


def tile_kernel(left_ref, right_ref, out_ref):
    right = jnp.concatenate([right_ref[0, 0, c] for c in range(8)], axis=1)
    out_ref[0, 0] = jnp.dot(
        left_ref[0, 0], right, preferred_element_type=jnp.float32
    ).astype(jnp.bfloat16)


def shards(hidden_stack, model_stack, tenant_weights, ranks, start_basis):
    f32, bf16 = jnp.float32, jnp.bfloat16
    shape = jax.ShapeDtypeStruct
    sem = pltpu.SemaphoreType.DMA
    gm, gh, mbuf, win = pl.pallas_call(
        gram_kernel,
        out_shape=[
            shape((8, 16, 384), f32), shape((8, 16, 384), f32),
            shape((32, 8, 1024), bf16), shape((32, 8, 512), bf16),
        ],
        in_specs=[ANY, ANY],
        out_specs=[VM] * 4,
        scratch_shapes=[
            pltpu.VMEM((32, 8, 3584), bf16),
            pltpu.VMEM((8, 16, 384), f32), pltpu.VMEM((8, 16, 384), f32),
            pltpu.VMEM((8, 16, 384), f32), pltpu.VMEM((8, 16, 384), f32),
            sem((12,)),
        ],
        compiler_params=pltpu.CompilerParams(
            collective_id=0, has_side_effects=True, vmem_limit_bytes=VMEM_BYTES
        ),
    )(hidden_stack, model_stack)
    left, right = pl.pallas_call(
        core_kernel,
        out_shape=[shape((4, SERVE_DEV, 128), bf16), shape((8, 128, 128), bf16)],
        in_specs=[VM, VM, VM, VM, SM, SM, VM],
        out_specs=[VM, VM],
        scratch_shapes=[
            pltpu.VMEM((256, 256), f32), pltpu.VMEM((256, 256), f32), pltpu.VMEM((256, 256), f32),
            pltpu.VMEM((256, 128), f32), pltpu.VMEM((512, 128), f32),
        ],
        compiler_params=pltpu.CompilerParams(vmem_limit_bytes=VMEM_BYTES),
    )(gm, gh, mbuf, win, tenant_weights, ranks, start_basis)
    lall, rall = pl.pallas_call(
        gather_kernel,
        out_shape=[shape((8, PROJ, SERVE_DEV, 128), bf16), shape((8, PROJ, 8, 128, 128), bf16)],
        in_specs=[ANY, ANY],
        out_specs=[ANY, ANY],
        scratch_shapes=[
            sem((2,)), sem((2,)), sem, sem,
            sem((2, 2, 4)), sem((2, 2, 4)), sem((3,)), sem((3,)),
            sem((2, 5, 2)), sem((2, 5, 2)), sem((2, 5, 2)), sem((2, 5, 2)),
        ],
        compiler_params=pltpu.CompilerParams(collective_id=1, has_side_effects=True),
    )(left, right)
    return pl.pallas_call(
        tile_kernel,
        grid=(8, PROJ),
        out_shape=shape((8, PROJ, SERVE_DEV, 1024), bf16),
        in_specs=[
            pl.BlockSpec((1, 1, SERVE_DEV, 128), lambda l, p: (l, p, 0, 0)),
            pl.BlockSpec((1, 1, 8, 128, 128), lambda l, p: (l, p, 0, 0, 0)),
        ],
        out_specs=pl.BlockSpec((1, 1, SERVE_DEV, 1024), lambda l, p: (l, p, 0, 0)),
    )(lall, rall)


def solution(mesh):
    in_specs = (
        P("layer", None, "row", None),
        P("layer", None, "row", None),
        P(),
        P(),
        P("layer", None, None),
    )
    out_specs = P(None, None, "row", "layer")
    return jax.shard_map(shards, mesh=mesh, in_specs=in_specs, out_specs=out_specs, check_vma=False)
```

```python
import functools
import jax
import jax.numpy as jnp
from jax import lax
from jax.experimental import pallas as pl
from jax.experimental.pallas import tpu as pltpu
from jax.sharding import PartitionSpec as P

ITERS = 3
SERVE_DEV = 64
MOST_RANK = 64
PROJ = 3
HI = lax.Precision.HIGHEST
MESH = pl.DeviceIdType.MESH
VM = pl.BlockSpec(memory_space=pltpu.VMEM)
ANY = pl.BlockSpec(memory_space=pl.ANY)
SM = pl.BlockSpec(memory_space=pltpu.SMEM)
VMEM_BYTES = 48 * 1024 * 1024


def dot_hi(a, b, dims):
    return lax.dot_general(a, b, (dims, ((), ())), precision=HI, preferred_element_type=jnp.float32)


def spread_lane(tile, lane):
    return jnp.broadcast_to(tile[:, lane:lane + 1], (8, 128))


def spread_row(tile, row):
    return jnp.broadcast_to(tile[row:row + 1, :], (8, 128))


def factor(matrix, need_upper, need_inverse):
    sub = lax.broadcasted_iota(jnp.int32, (8, 128), 0)
    lane = lax.broadcasted_iota(jnp.int32, (8, 128), 1)
    rows = [matrix[8 * k:8 * k + 8, :] for k in range(16)]
    inverse = [jnp.where(lane == sub + 8 * k, 1.0, 0.0).astype(jnp.float32) for k in range(16)]
    upper_rows, inverse_rows = [], []
    for k in range(16):
        panel, ipanel = rows[k], inverse[k]
        cols = [spread_lane(panel, 8 * k + c) for c in range(8)]
        raw, iraw, diag = panel, ipanel, panel
        for j in range(8):
            pivot = spread_row(cols[j], j)
            recip = 1.0 / pivot
            scaled = cols[j] * recip
            here = sub == j
            prow = spread_row(panel, j)
            irow = spread_row(ipanel, j)
            raw = jnp.where(here, prow, raw)
            iraw = jnp.where(here, irow, iraw)
            diag = jnp.where(here, pivot, diag)
            panel = jnp.where(here, prow * recip, panel - scaled * prow)
            if need_inverse:
                ipanel = jnp.where(here, irow * recip, ipanel - scaled * irow)
            for c in range(j + 1, 8):
                crow = spread_row(cols[c], j)
                cols[c] = jnp.where(here, crow * recip, cols[c] - scaled * crow)
        root = lax.rsqrt(diag)
        upper_rows.append(raw * root)
        inverse_rows.append(iraw * root)
        prows = [spread_row(panel, c) for c in range(8)]
        irows = [spread_row(ipanel, c) for c in range(8)]
        for i in range(k + 1, 16):
            coef = [spread_lane(rows[i], 8 * k + c) for c in range(8)]
            rows[i] = rows[i] - sum(coef[c] * prows[c] for c in range(8))
            if need_inverse:
                inverse[i] = inverse[i] - sum(coef[c] * irows[c] for c in range(8))
    out = []
    if need_upper:
        rowi = lax.broadcasted_iota(jnp.int32, (128, 128), 0)
        coli = lax.broadcasted_iota(jnp.int32, (128, 128), 1)
        up = jnp.concatenate(upper_rows, axis=0)
        out.append(jnp.where(coli >= rowi, up, 0.0))
    if need_inverse:
        out.append(jnp.concatenate(inverse_rows, axis=0))
    return out


def place():
    layer = lax.axis_index("layer")
    row = lax.axis_index("row")
    return layer, row, row // 4, row % 4


def remote(src, dst, send, recv, layer, row):
    return pltpu.make_async_remote_copy(
        src_ref=src, dst_ref=dst, send_sem=send, recv_sem=recv,
        device_id=(layer, row), device_id_type=MESH,
    )


def wait_bytes(ref, sem):
    pltpu.make_async_copy(ref, ref, sem).wait()


def pack_gram(buf, part):
    ranks = buf.shape[0] * buf.shape[1]
    factors = buf[...].astype(jnp.float32).reshape(ranks, buf.shape[2]).astype(jnp.bfloat16)
    gram = lax.dot_general(
        factors, factors, (((1,), (1,)), ((), ())), preferred_element_type=jnp.float32
    )
    part[:, :, 0:128] = gram[0:128, 0:128].reshape(8, 16, 128)
    part[:, :, 128:384] = gram[128:256, :].reshape(8, 16, 256)


def start_reduce(part, slots, send, recv, layer, z, x):
    def one(k, carry):
        to = (z + k) % 8
        remote(part.at[to], slots.at[z], send, recv, layer, to * 4 + x).start()
        return carry

    lax.fori_loop(1, 8, one, 0)
    slots[pl.ds(z, 1)] = part[pl.ds(z, 1)]


def start_share(slots, out, send, recv, send2, recv2, layer, z, x):
    wait_bytes(slots.at[pl.ds(0, 7)], recv)
    wait_bytes(slots.at[pl.ds(0, 7)], send)
    total = slots[0]
    for k in range(1, 8):
        total = total + slots[k]
    out[pl.ds(z, 1)] = total[None]

    def one(k, carry):
        to = (z + k) % 8
        remote(out.at[z], out.at[z], send2, recv2, layer, to * 4 + x).start()
        return carry

    lax.fori_loop(1, 8, one, 0)


def end_share(out, send2, recv2):
    wait_bytes(out.at[pl.ds(0, 7)], recv2)
    wait_bytes(out.at[pl.ds(0, 7)], send2)


def core_kernel(f_ref, m_ref, weights_ref, ranks_ref, start_ref, left_ref, right_ref, mbuf, fbuf,
                part_m, part_h, slots_m, slots_h, gm_ref, gh_ref,
                lower_s, upper_s, pulled_map, basis_s, both_s, sems):
    layer, row, z, x = place()
    barrier = pltpu.get_barrier_semaphore()

    def greet(k, carry):
        pl.semaphore_signal(barrier, inc=1, device_id=(layer, (row + k) % 32), device_id_type=MESH)
        return carry

    lax.fori_loop(1, 32, greet, 0)
    pl.semaphore_wait(barrier, 31)
    mwide, fwide = mbuf.shape[2], fbuf.shape[2]

    def pieces(src_ref, wide, to):
        column = pl.multiple_of((to // 4) * wide, 128)
        return src_ref.at[0, to % 4, :, pl.ds(column, wide)]

    for src_ref, buf, wide, base in ((m_ref, mbuf, mwide, 0), (f_ref, fbuf, fwide, 2)):
        def send(k, carry):
            to = (row + k) % 32

            @pl.when(to % 4 < PROJ)
            def _():
                remote(
                    pieces(src_ref, wide, to), buf.at[row], sems.at[base], sems.at[base + 1], layer, to
                ).start()

            return carry

        lax.fori_loop(1, 32, send, 0)

        @pl.when(x < PROJ)
        def _():
            pltpu.make_async_copy(pieces(src_ref, wide, row), buf.at[row], sems.at[base + 1]).start()

    @pl.when(x < PROJ)
    def _():
        wait_bytes(mbuf, sems.at[1])
        pack_gram(mbuf, part_m)
        start_reduce(part_m, slots_m, sems.at[4], sems.at[5], layer, z, x)
        start_share(slots_m, gm_ref, sems.at[4], sems.at[5], sems.at[6], sems.at[7], layer, z, x)
        end_share(gm_ref, sems.at[6], sems.at[7])
        lower_factor(gm_ref, weights_ref, ranks_ref, lower_s, upper_s)
        wait_bytes(fbuf, sems.at[3])
        pack_gram(fbuf, part_h)
        start_reduce(part_h, slots_h, sems.at[8], sems.at[9], layer, z, x)
        start_share(slots_h, gh_ref, sems.at[8], sems.at[9], sems.at[10], sems.at[11], layer, z, x)
        end_share(gh_ref, sems.at[10], sems.at[11])
        iterate(gh_ref, start_ref, lower_s, upper_s, pulled_map, basis_s, both_s)
        truncated(mbuf, fbuf, weights_ref, ranks_ref, lower_s, basis_s, both_s, left_ref, right_ref)
        wait_bytes(mbuf.at[pl.ds(0, 23)], sems.at[0])
        wait_bytes(fbuf.at[pl.ds(0, 23)], sems.at[2])

    @pl.when(x >= PROJ)
    def _():
        wait_bytes(mbuf.at[pl.ds(0, 24)], sems.at[0])
        wait_bytes(fbuf.at[pl.ds(0, 24)], sems.at[2])


def column_scale(ranks_ref, weights_ref, index):
    total = jnp.zeros(index.shape, jnp.float32)
    begin = 0
    for t in range(8):
        end = begin + ranks_ref[t]
        rank = jnp.full(index.shape, ranks_ref[t].astype(jnp.float32))
        factor_t = weights_ref[t] * jnp.sqrt(MOST_RANK / rank)
        total = jnp.where((index >= begin) & (index < end), factor_t, total)
        begin = end
    return total


def lower_factor(gm_ref, weights_ref, ranks_ref, lower_s, upper_s):
    scale_col = column_scale(ranks_ref, weights_ref, lax.broadcasted_iota(jnp.int32, (256, 1), 0))
    scale_row = column_scale(ranks_ref, weights_ref, lax.broadcasted_iota(jnp.int32, (1, 256), 1))
    packed = gm_ref[...].reshape(128, 384)
    first = packed[:, 0:128] * (scale_col[0:128] * scale_row[:, 0:128])
    cross = packed[:, 128:256] * (scale_col[128:256] * scale_row[:, 0:128])
    last = packed[:, 256:384] * (scale_col[128:256] * scale_row[:, 128:256])
    upper_first, inverse_first = factor(first, True, True)
    low = dot_hi(cross, inverse_first, ((1,), (1,)))
    (upper_last,) = factor(last - dot_hi(low, low, ((1,), (1,))), True, False)
    zero = jnp.zeros((128, 128), jnp.float32)
    upper_s[0:128, 0:128] = upper_first
    upper_s[0:128, 128:256] = low.T
    upper_s[128:256, 0:128] = zero
    upper_s[128:256, 128:256] = upper_last
    lower_s[0:128, 0:128] = upper_first.T
    lower_s[0:128, 128:256] = zero
    lower_s[128:256, 0:128] = low
    lower_s[128:256, 128:256] = upper_last.T


def iterate(gh_ref, start_ref, lower_s, upper_s, pulled_map, basis_s, both_s):
    packed = gh_ref[...].reshape(128, 384)
    hidden = jnp.concatenate(
        [
            jnp.concatenate([packed[:, 0:128], packed[:, 128:256].T], axis=1),
            packed[:, 128:384],
        ],
        axis=0,
    )
    pulled_map[...] = dot_hi(hidden, lower_s[...], ((1,), (0,)))
    basis_s[...] = start_ref[0]

    def sweep(_, carry):
        pushed = dot_hi(pulled_map[...], basis_s[...], ((1,), (0,)))
        both_s[0:256, :] = dot_hi(upper_s[...], pushed, ((1,), (0,)))
        both_s[256:512, :] = pushed

        def one_pass(_, inner):
            raised = both_s[0:256, :]
            (inverse,) = factor(dot_hi(raised, raised, ((0,), (0,))), False, True)
            both_s[...] = dot_hi(both_s[...], inverse, ((1,), (1,)))
            return inner

        lax.fori_loop(0, 2, one_pass, 0)
        basis_s[...] = both_s[0:256, :]
        return carry

    lax.fori_loop(0, ITERS, sweep, 0)


def truncated(mbuf, fbuf, weights_ref, ranks_ref, lower_s, basis_s, both_s, left_ref, right_ref):
    scale_col = column_scale(ranks_ref, weights_ref, lax.broadcasted_iota(jnp.int32, (256, 1), 0))
    lifted = dot_hi(lower_s[...], basis_s[...], ((1,), (0,)))
    pulled = scale_col * both_s[256:512, :]
    for j in range(4):
        window = fbuf[:, :, 896 * j:896 * j + 128].astype(jnp.float32).reshape(256, 128)
        left = dot_hi(window, lifted, ((0,), (0,)))
        left_ref[j] = left[0:SERVE_DEV].astype(jnp.bfloat16)
    model = mbuf[...].astype(jnp.float32).reshape(256, 1024)
    right = dot_hi(pulled, model, ((0,), (0,))).astype(jnp.bfloat16)
    for c in range(8):
        right_ref[c] = right[:, 128 * c:128 * c + 128]


def gather_kernel(left_ref, right_ref, lall, rall, in_send, in_recv, left_send, left_recv,
                  ring_send, ring_recv, side_send, side_recv, wide_send, wide_recv, pass_send, pass_recv):
    layer, row, z, x = place()
    barrier = pltpu.get_barrier_semaphore()

    def greet(to_layer, to_row):
        pl.semaphore_signal(barrier, inc=1, device_id=(to_layer, to_row), device_id_type=MESH)

    def row_at(to_z, to_x):
        return (to_z % 8) * 4 + to_x % 4

    owner = layer == z
    real = x < PROJ
    for k in range(1, 8):
        greet((layer + k) % 8, row)
    for k in range(1, 4):
        greet(layer, row_at(z, x + k))
    greet(layer, row_at(z + 1, x))
    greet(layer, row_at(z + 7, x))
    @pl.when(real & (layer != z))
    def _():
        for l in range(8):
            ring_peer = (layer == (z + 1) % 8) | (layer == (z + 7) % 8)

            @pl.when(jnp.logical_not(ring_peer & (layer == l)))
            def _():
                greet(l, row_at(layer, x))

    pl.semaphore_wait(barrier, 12 + jnp.where(real, 7 - jnp.where(owner, 2, 0), 0))

    @pl.when(real)
    def _():
        for c in range(8):
            mine = rall.at[layer, x, c]

            @pl.when(owner & (z == c))
            def _():
                pltpu.make_async_copy(right_ref.at[c], mine, in_recv.at[0]).start()

            @pl.when(jnp.logical_not(owner & (z == c)))
            def _():
                remote(right_ref.at[c], mine, in_send.at[0], in_recv.at[0], z, row_at(c, x)).start()

        for k in range(1, 4):
            to = (x + k) % 4
            remote(left_ref.at[to], lall.at[layer, x], in_send.at[1], in_recv.at[1],
                   layer, row_at(z, to)).start()
        pltpu.make_async_copy(left_ref.at[x], lall.at[layer, x], in_recv.at[1]).start()

    wait_bytes(lall.at[layer], in_recv.at[1])
    for k in range(1, 8):
        to = (layer + k) % 8
        remote(lall.at[layer], lall.at[layer], left_send, left_recv, to, row).start()

    def shard(low, high, p, c):
        return rall.at[pl.ds(low, high - low), p, c % 8]

    def thick(low, high, c):
        return rall.at[pl.ds(low, high - low), :, c % 8]

    def ring(step, group):
        low = 4 * group
        cut = thick if group else lambda a, b, c: shard(a, b, x, c)
        up_high = low + (4 if step < 3 else 2)
        down_low = low + (0 if step < 3 else 2)
        up = remote(cut(low, up_high, z + 8 - step), cut(low, up_high, z + 8 - step),
                    ring_send.at[group, 0, step], ring_recv.at[group, 0, step], layer, row_at(z + 1, x))
        down = remote(cut(down_low, low + 4, z + step), cut(down_low, low + 4, z + step),
                      ring_send.at[group, 1, step], ring_recv.at[group, 1, step], layer, row_at(z + 7, x))
        return up, down

    def ring_got(step, group):
        low = 4 * group
        cut = thick if group else lambda a, b, c: shard(a, b, x, c)
        up_high = low + (4 if step < 3 else 2)
        down_low = low + (0 if step < 3 else 2)
        wait_bytes(cut(low, up_high, z + 7 - step), ring_recv.at[group, 0, step])
        wait_bytes(cut(down_low, low + 4, z + 1 + step), ring_recv.at[group, 1, step])

    def columns(turn):
        if turn == 0:
            return (z,)
        if turn == 4:
            return (z + 4,)
        return (z + 8 - turn, z + turn)

    def widen(turn):
        for n, c in enumerate(columns(turn)):
            piece = shard(0, 4, x, c)
            remote(piece, piece, wide_send.at[0, turn, n], wide_recv.at[0, turn, n],
                   layer, row_at(z, x + 1)).start()
            remote(piece, piece, wide_send.at[1, turn, n], wide_recv.at[1, turn, n],
                   layer, row_at(z, x + 3)).start()

    def widen_sent(turn):
        for n, c in enumerate(columns(turn)):
            piece = shard(0, 4, x, c)
            wait_bytes(piece, wide_send.at[0, turn, n])
            wait_bytes(piece, wide_send.at[1, turn, n])

    before, after = (x + 3) % 4, (x + 1) % 4

    def relay(turn):
        for n, c in enumerate(columns(turn)):
            @pl.when(before < PROJ)
            def _():
                wait_bytes(shard(0, 4, before, c), wide_recv.at[0, turn, n])
                piece = shard(0, 2, before, c)
                remote(piece, piece, pass_send.at[0, turn, n], pass_recv.at[0, turn, n],
                       layer, row_at(z, x + 1)).start()

            @pl.when(after < PROJ)
            def _():
                wait_bytes(shard(0, 4, after, c), wide_recv.at[1, turn, n])
                piece = shard(2, 4, after, c)
                remote(piece, piece, pass_send.at[1, turn, n], pass_recv.at[1, turn, n],
                       layer, row_at(z, x + 3)).start()

    def relay_end(turn):
        far = (x + 2) % 4
        for n, c in enumerate(columns(turn)):
            @pl.when(before < PROJ)
            def _():
                wait_bytes(shard(0, 2, before, c), pass_send.at[0, turn, n])

            @pl.when(after < PROJ)
            def _():
                wait_bytes(shard(2, 4, after, c), pass_send.at[1, turn, n])

            @pl.when(far < PROJ)
            def _():
                wait_bytes(shard(0, 2, far, c), pass_recv.at[0, turn, n])
                wait_bytes(shard(2, 4, far, c), pass_recv.at[1, turn, n])

    @pl.when(real)
    def _():
        wait_bytes(rall.at[:, x, z], in_recv.at[0])
        piece = shard(4, 8, x, z)
        for k in range(1, 4):
            remote(piece, piece, side_send.at[k - 1], side_recv.at[k - 1], layer, row_at(z, x + k)).start()
        for copy in ring(0, 0):
            copy.start()
        widen(0)

    for k in range(1, 4):
        source = (x + 4 - k) % 4

        @pl.when(source < PROJ)
        def _():
            wait_bytes(shard(4, 8, source, z), side_recv.at[k - 1])

    for copy in ring(0, 1):
        copy.start()
    for step in range(4):
        @pl.when(real)
        def _():
            ring_got(step, 0)
            if step < 3:
                for copy in ring(step + 1, 0):
                    copy.start()
            widen(step + 1)

        ring_got(step, 1)
        if step < 3:
            for copy in ring(step + 1, 1):
                copy.start()
        relay(step)
    relay(4)
    for turn in range(5):
        relay_end(turn)
    for step in range(4):
        for copy in ring(step, 1):
            copy.wait_send()

    @pl.when(real)
    def _():
        for turn in range(5):
            widen_sent(turn)
        for step in range(4):
            for copy in ring(step, 0):
                copy.wait_send()
        piece = shard(4, 8, x, z)
        for k in range(1, 4):
            wait_bytes(piece, side_send.at[k - 1])

        @pl.when(owner)
        def _():
            wait_bytes(right_ref.at[pl.ds(0, 7)], in_send.at[0])

        @pl.when(jnp.logical_not(owner))
        def _():
            wait_bytes(right_ref, in_send.at[0])

        wait_bytes(left_ref.at[pl.ds(0, 3)], in_send.at[1])

    wait_bytes(lall.at[pl.ds(0, 7)], left_send)
    wait_bytes(lall.at[pl.ds(0, 7)], left_recv)


def tile_kernel(left_ref, right_ref, out_ref):
    for p in range(PROJ):
        right = jnp.concatenate([right_ref[0, p, c] for c in range(8)], axis=1)
        out_ref[0, p] = jnp.dot(
            left_ref[0, p], right, preferred_element_type=jnp.float32
        ).astype(jnp.bfloat16)


def shards(hidden_stack, model_stack, tenant_weights, ranks, start_basis):
    f32, bf16 = jnp.float32, jnp.bfloat16
    shape = jax.ShapeDtypeStruct
    sem = pltpu.SemaphoreType.DMA
    gram = pltpu.VMEM((8, 16, 384), f32)
    left, right = pl.pallas_call(
        core_kernel,
        out_shape=[shape((4, SERVE_DEV, 128), bf16), shape((8, 128, 128), bf16)],
        in_specs=[ANY, ANY, SM, SM, VM],
        out_specs=[VM, VM],
        scratch_shapes=[
            pltpu.VMEM((32, 8, 1024), bf16), pltpu.VMEM((32, 8, 3584), bf16),
            gram, gram, gram, gram, gram, gram,
            pltpu.VMEM((256, 256), f32), pltpu.VMEM((256, 256), f32), pltpu.VMEM((256, 256), f32),
            pltpu.VMEM((256, 128), f32), pltpu.VMEM((512, 128), f32),
            sem((12,)),
        ],
        compiler_params=pltpu.CompilerParams(
            collective_id=0, has_side_effects=True, vmem_limit_bytes=VMEM_BYTES
        ),
    )(hidden_stack, model_stack, tenant_weights, ranks, start_basis)
    lall, rall = pl.pallas_call(
        gather_kernel,
        out_shape=[shape((8, PROJ, SERVE_DEV, 128), bf16), shape((8, PROJ, 8, 128, 128), bf16)],
        in_specs=[ANY, ANY],
        out_specs=[ANY, ANY],
        scratch_shapes=[
            sem((2,)), sem((2,)), sem, sem,
            sem((2, 2, 4)), sem((2, 2, 4)), sem((3,)), sem((3,)),
            sem((2, 5, 2)), sem((2, 5, 2)), sem((2, 5, 2)), sem((2, 5, 2)),
        ],
        compiler_params=pltpu.CompilerParams(collective_id=1, has_side_effects=True),
    )(left, right)
    return pl.pallas_call(
        tile_kernel,
        grid=(8,),
        out_shape=shape((8, PROJ, SERVE_DEV, 1024), bf16),
        in_specs=[
            pl.BlockSpec((1, PROJ, SERVE_DEV, 128), lambda l: (l, 0, 0, 0)),
            pl.BlockSpec((1, PROJ, 8, 128, 128), lambda l: (l, 0, 0, 0, 0)),
        ],
        out_specs=pl.BlockSpec((1, PROJ, SERVE_DEV, 1024), lambda l: (l, 0, 0, 0)),
    )(lall, rall)


def solution(mesh):
    in_specs = (
        P("layer", None, "row", None),
        P("layer", None, "row", None),
        P(),
        P(),
        P("layer", None, None),
    )
    out_specs = P(None, None, "row", "layer")
    return jax.shard_map(shards, mesh=mesh, in_specs=in_specs, out_specs=out_specs, check_vma=False)
```

```python
import functools
import jax
import jax.numpy as jnp
from jax import lax
from jax.experimental import pallas as pl
from jax.experimental.pallas import tpu as pltpu
from jax.sharding import PartitionSpec as P

ITERS = 3
SERVE_DEV = 64
MOST_RANK = 64
PROJ = 3
SPLIT = 5
HI = lax.Precision.HIGHEST
MESH = pl.DeviceIdType.MESH
VM = pl.BlockSpec(memory_space=pltpu.VMEM)
ANY = pl.BlockSpec(memory_space=pl.ANY)
SM = pl.BlockSpec(memory_space=pltpu.SMEM)
VMEM_BYTES = 48 * 1024 * 1024


def dot_hi(a, b, dims):
    return lax.dot_general(a, b, (dims, ((), ())), precision=HI, preferred_element_type=jnp.float32)


def spread_lane(tile, lane):
    return jnp.broadcast_to(tile[:, lane:lane + 1], (8, 128))


def spread_row(tile, row):
    return jnp.broadcast_to(tile[row:row + 1, :], (8, 128))


def factor(matrix, need_upper, need_inverse):
    sub = lax.broadcasted_iota(jnp.int32, (8, 128), 0)
    lane = lax.broadcasted_iota(jnp.int32, (8, 128), 1)
    rows = [matrix[8 * k:8 * k + 8, :] for k in range(16)]
    inverse = [jnp.where(lane == sub + 8 * k, 1.0, 0.0).astype(jnp.float32) for k in range(16)]
    upper_rows, inverse_rows = [], []
    for k in range(16):
        panel, ipanel = rows[k], inverse[k]
        cols = [spread_lane(panel, 8 * k + c) for c in range(8)]
        raw, iraw, diag = panel, ipanel, panel
        for j in range(8):
            pivot = spread_row(cols[j], j)
            recip = 1.0 / pivot
            scaled = cols[j] * recip
            here = sub == j
            prow = spread_row(panel, j)
            irow = spread_row(ipanel, j)
            raw = jnp.where(here, prow, raw)
            iraw = jnp.where(here, irow, iraw)
            diag = jnp.where(here, pivot, diag)
            panel = jnp.where(here, prow * recip, panel - scaled * prow)
            if need_inverse:
                ipanel = jnp.where(here, irow * recip, ipanel - scaled * irow)
            for c in range(j + 1, 8):
                crow = spread_row(cols[c], j)
                cols[c] = jnp.where(here, crow * recip, cols[c] - scaled * crow)
        root = lax.rsqrt(diag)
        upper_rows.append(raw * root)
        inverse_rows.append(iraw * root)
        prows = [spread_row(panel, c) for c in range(8)]
        irows = [spread_row(ipanel, c) for c in range(8)]
        for i in range(k + 1, 16):
            coef = [spread_lane(rows[i], 8 * k + c) for c in range(8)]
            rows[i] = rows[i] - sum(coef[c] * prows[c] for c in range(8))
            if need_inverse:
                inverse[i] = inverse[i] - sum(coef[c] * irows[c] for c in range(8))
    out = []
    if need_upper:
        rowi = lax.broadcasted_iota(jnp.int32, (128, 128), 0)
        coli = lax.broadcasted_iota(jnp.int32, (128, 128), 1)
        up = jnp.concatenate(upper_rows, axis=0)
        out.append(jnp.where(coli >= rowi, up, 0.0))
    if need_inverse:
        out.append(jnp.concatenate(inverse_rows, axis=0))
    return out


def place():
    layer = lax.axis_index("layer")
    row = lax.axis_index("row")
    return layer, row, row // 4, row % 4


def remote(src, dst, send, recv, layer, row):
    return pltpu.make_async_remote_copy(
        src_ref=src, dst_ref=dst, send_sem=send, recv_sem=recv,
        device_id=(layer, row), device_id_type=MESH,
    )


def wait_bytes(ref, sem):
    pltpu.make_async_copy(ref, ref, sem).wait()


def pack_gram(buf, part):
    ranks = buf.shape[0] * buf.shape[1]
    factors = buf[...].astype(jnp.float32).reshape(ranks, buf.shape[2]).astype(jnp.bfloat16)
    gram = lax.dot_general(
        factors, factors, (((1,), (1,)), ((), ())), preferred_element_type=jnp.float32
    )
    part[:, :, 0:128] = gram[0:128, 0:128].reshape(8, 16, 128)
    part[:, :, 128:384] = gram[128:256, :].reshape(8, 16, 256)


def start_reduce(part, slots, send, recv, layer, z, x):
    def one(k, carry):
        to = (z + k) % 8
        remote(part.at[to], slots.at[z], send, recv, layer, to * 4 + x).start()
        return carry

    lax.fori_loop(1, 8, one, 0)
    slots[pl.ds(z, 1)] = part[pl.ds(z, 1)]


def start_share(slots, out, send, recv, send2, recv2, layer, z, x):
    wait_bytes(slots.at[pl.ds(0, 7)], recv)
    wait_bytes(slots.at[pl.ds(0, 7)], send)
    total = slots[0]
    for k in range(1, 8):
        total = total + slots[k]
    out[pl.ds(z, 1)] = total[None]

    def one(k, carry):
        to = (z + k) % 8
        remote(out.at[z], out.at[z], send2, recv2, layer, to * 4 + x).start()
        return carry

    lax.fori_loop(1, 8, one, 0)


def end_share(out, send2, recv2):
    wait_bytes(out.at[pl.ds(0, 7)], recv2)
    wait_bytes(out.at[pl.ds(0, 7)], send2)


def column_scale(ranks_ref, weights_ref, index):
    total = jnp.zeros(index.shape, jnp.float32)
    begin = 0
    for t in range(8):
        end = begin + ranks_ref[t]
        rank = jnp.full(index.shape, ranks_ref[t].astype(jnp.float32))
        factor_t = weights_ref[t] * jnp.sqrt(MOST_RANK / rank)
        total = jnp.where((index >= begin) & (index < end), factor_t, total)
        begin = end
    return total


def lower_factor(gm_ref, weights_ref, ranks_ref, lower_s, upper_s):
    scale_col = column_scale(ranks_ref, weights_ref, lax.broadcasted_iota(jnp.int32, (256, 1), 0))
    scale_row = column_scale(ranks_ref, weights_ref, lax.broadcasted_iota(jnp.int32, (1, 256), 1))
    packed = gm_ref[...].reshape(128, 384)
    first = packed[:, 0:128] * (scale_col[0:128] * scale_row[:, 0:128])
    cross = packed[:, 128:256] * (scale_col[128:256] * scale_row[:, 0:128])
    last = packed[:, 256:384] * (scale_col[128:256] * scale_row[:, 128:256])
    upper_first, inverse_first = factor(first, True, True)
    low = dot_hi(cross, inverse_first, ((1,), (1,)))
    (upper_last,) = factor(last - dot_hi(low, low, ((1,), (1,))), True, False)
    zero = jnp.zeros((128, 128), jnp.float32)
    upper_s[0:128, 0:128] = upper_first
    upper_s[0:128, 128:256] = low.T
    upper_s[128:256, 0:128] = zero
    upper_s[128:256, 128:256] = upper_last
    lower_s[0:128, 0:128] = upper_first.T
    lower_s[0:128, 128:256] = zero
    lower_s[128:256, 0:128] = low
    lower_s[128:256, 128:256] = upper_last.T


def hidden_map(gh_ref, lower_s, pulled_map):
    packed = gh_ref[...].reshape(128, 384)
    hidden = jnp.concatenate(
        [
            jnp.concatenate([packed[:, 0:128], packed[:, 128:256].T], axis=1),
            packed[:, 128:384],
        ],
        axis=0,
    )
    pulled_map[...] = dot_hi(hidden, lower_s[...], ((1,), (0,)))


def start_sweep(upper_s, pulled_map, both_s):
    pushed = dot_hi(pulled_map[...], both_s[0:256, :], ((1,), (0,)))
    both_s[0:256, :] = dot_hi(upper_s[...], pushed, ((1,), (0,)))
    both_s[256:512, :] = pushed


def one_pass(both_s):
    raised = both_s[0:256, :]
    (inverse,) = factor(dot_hi(raised, raised, ((0,), (0,))), False, True)
    both_s[...] = dot_hi(both_s[...], inverse, ((1,), (1,)))


def window_maps(fbuf, weights_ref, ranks_ref, lower_s, both_s, maps):
    scale_col = column_scale(ranks_ref, weights_ref, lax.broadcasted_iota(jnp.int32, (256, 1), 0))
    lifted = dot_hi(lower_s[...], both_s[0:256, :], ((1,), (0,)))
    pulled = scale_col * both_s[256:512, :]
    for j in range(4):
        window = fbuf[:, :, 896 * j:896 * j + 128].astype(jnp.float32).reshape(256, 128)
        left = dot_hi(window, lifted, ((0,), (0,)))
        left = left[0:SERVE_DEV].astype(jnp.bfloat16).astype(jnp.float32)
        maps[j] = dot_hi(left, pulled, ((1,), (1,))).astype(jnp.bfloat16)


def merge_kernel(f_ref, m_ref, weights_ref, ranks_ref, start_ref, wall, mall, mbuf, fbuf,
                 part_m, part_h, slots_m, slots_h, gm_ref, gh_ref,
                 lower_s, upper_s, pulled_map, both_s, maps, sems,
                 ring_send, ring_recv, side_send, side_recv, wide_send, wide_recv, pass_send, pass_recv,
                 over_send, over_recv):
    layer, row, z, x = place()
    real = x < PROJ
    barrier = pltpu.get_barrier_semaphore()

    def greet(k, carry):
        pl.semaphore_signal(barrier, inc=1, device_id=(layer, (row + k) % 32), device_id_type=MESH)
        return carry

    lax.fori_loop(1, 32, greet, 0)
    for k in range(1, 8):
        pl.semaphore_signal(barrier, inc=1, device_id=((layer + k) % 8, row), device_id_type=MESH)
    pl.semaphore_wait(barrier, 38)

    def row_at(to_z, to_x):
        return (to_z % 8) * 4 + to_x % 4

    mwide, fwide = mbuf.shape[2], fbuf.shape[2]

    def pieces(src_ref, wide, to):
        column = pl.multiple_of((to // 4) * wide, 128)
        return src_ref.at[0, to % 4, :, pl.ds(column, wide)]

    def scatter(src_ref, buf, wide, base, low, high):
        def send(k, carry):
            to = (row + k) % 32

            @pl.when(to % 4 < PROJ)
            def _():
                remote(
                    pieces(src_ref, wide, to), buf.at[row], sems.at[base], sems.at[base + 1], layer, to
                ).start()

            return carry

        lax.fori_loop(low, high, send, 0)

    def keep(src_ref, buf, wide, base):
        pltpu.make_async_copy(pieces(src_ref, wide, row), buf.at[row], sems.at[base + 1]).start()

    def owned(to):
        return m_ref.at[0, :, :, pl.ds(pl.multiple_of(to * 1024, 128), 1024)]

    def shard(p, c, low=0, wide=1024):
        return mall.at[pl.ds(0, SPLIT), :, (c % 8) * 4 + p, :, pl.ds(low, wide)]

    def thick(c, low=0, count=4):
        return mall.at[pl.ds(SPLIT, 8 - SPLIT), :, pl.ds((c % 8) * 4 + low, count)]

    def halves(step, group, up_c, down_c):
        if group:
            return (thick(up_c), thick(down_c)) if step < 3 else (thick(up_c, 0, 2), thick(down_c, 2, 2))
        if step < 3:
            return shard(x, up_c), shard(x, down_c)
        return shard(x, up_c, 0, 512), shard(x, down_c, 512, 512)

    def ring(step, group):
        up, down = halves(step, group, z + 8 - step, z + step)
        return (
            remote(up, up, ring_send.at[group, 0, step], ring_recv.at[group, 0, step], layer, row_at(z + 1, x)),
            remote(down, down, ring_send.at[group, 1, step], ring_recv.at[group, 1, step],
                   layer, row_at(z + 7, x)),
        )

    def ring_start(step, group):
        for copy in ring(step, group):
            copy.start()

    def ring_got(step, group):
        up, down = halves(step, group, z + 7 - step, z + 1 + step)
        wait_bytes(up, ring_recv.at[group, 0, step])
        wait_bytes(down, ring_recv.at[group, 1, step])

    def columns(turn):
        if turn == 0:
            return (z,)
        if turn == 4:
            return (z + 4,)
        return (z + 8 - turn, z + turn)

    def widen(turn):
        for n, c in enumerate(columns(turn)):
            piece = shard(x, c)
            for way in range(2):
                remote(piece, piece, wide_send.at[way, turn, n], wide_recv.at[way, turn, n],
                       layer, row_at(z, x + 1 + 2 * way)).start()

    before, after, far = (x + 3) % 4, (x + 1) % 4, (x + 2) % 4

    def relay(turn):
        for n, c in enumerate(columns(turn)):
            for way, source in enumerate((before, after)):
                wait_bytes(shard(source, c), wide_recv.at[way, turn, n])
                piece = shard(source, c, 512 * way, 512)
                remote(piece, piece, pass_send.at[way, turn, n], pass_recv.at[way, turn, n],
                       layer, row_at(z, x + 1 + 2 * way)).start()

    def relay_end(turn):
        for n, c in enumerate(columns(turn)):
            for way, source in enumerate((before, after)):
                wait_bytes(shard(x, c), wide_send.at[way, turn, n])
                wait_bytes(shard(source, c, 512 * way, 512), pass_send.at[way, turn, n])
                wait_bytes(shard(far, c, 512 * way, 512), pass_recv.at[way, turn, n])

    def narrow(k):
        return mall.at[pl.ds(SPLIT, 8 - SPLIT), :, row_at(z, x + k)]

    def ring_a(step):
        ring_got(step, 0)
        if step < 3:
            ring_start(step + 1, 0)
        widen(step + 1)

    def ring_b(step):
        ring_got(step, 1)
        if step < 3:
            ring_start(step + 1, 1)

    scatter(m_ref, mbuf, mwide, 0, 1, 32)
    for k in range(1, 8):
        to = (layer + k) % 8
        remote(owned(to), mall.at[layer, :, row], sems.at[12], sems.at[13], to, row).start()
    pltpu.make_async_copy(owned(layer), mall.at[layer, :, row], sems.at[13]).start()
    scatter(f_ref, fbuf, fwide, 2, 1, 11)

    @pl.when(real)
    def _():
        keep(m_ref, mbuf, mwide, 0)
        keep(f_ref, fbuf, fwide, 2)
        wait_bytes(mbuf, sems.at[1])
        pack_gram(mbuf, part_m)
        start_reduce(part_m, slots_m, sems.at[4], sems.at[5], layer, z, x)

    scatter(f_ref, fbuf, fwide, 2, 11, 21)

    @pl.when(real)
    def _():
        start_share(slots_m, gm_ref, sems.at[4], sems.at[5], sems.at[6], sems.at[7], layer, z, x)

    scatter(f_ref, fbuf, fwide, 2, 21, 32)
    wait_bytes(mall.at[:, :, row], sems.at[13])
    for k in range(1, 4):
        remote(narrow(0), narrow(0), side_send.at[k - 1], side_recv.at[k - 1], layer, row_at(z, x + k)).start()
    widen(0)

    @pl.when(real)
    def _():
        end_share(gm_ref, sems.at[6], sems.at[7])
        lower_factor(gm_ref, weights_ref, ranks_ref, lower_s, upper_s)
        wait_bytes(fbuf, sems.at[3])
        wait_bytes(mbuf.at[pl.ds(0, 23)], sems.at[0])
        wait_bytes(fbuf.at[pl.ds(0, 23)], sems.at[2])

    @pl.when(jnp.logical_not(real))
    def _():
        wait_bytes(mbuf.at[pl.ds(0, 24)], sems.at[0])
        wait_bytes(fbuf.at[pl.ds(0, 24)], sems.at[2])

    ring_start(0, 0)

    @pl.when(real)
    def _():
        pack_gram(fbuf, part_h)
        start_reduce(part_h, slots_h, sems.at[8], sems.at[9], layer, z, x)
        start_share(slots_h, gh_ref, sems.at[8], sems.at[9], sems.at[10], sems.at[11], layer, z, x)
        end_share(gh_ref, sems.at[10], sems.at[11])
        hidden_map(gh_ref, lower_s, pulled_map)
        both_s[0:256, :] = start_ref[0]

    def stage(i, carry):
        @pl.when(i == 0)
        def _():
            ring_a(0)
            for k in range(1, 4):
                wait_bytes(narrow(4 - k), side_recv.at[k - 1])
            ring_start(0, 1)

        @pl.when(i == 1)
        def _():
            ring_a(1)
            relay(0)

        @pl.when(i == 2)
        def _():
            relay(1)

        @pl.when(i == 3)
        def _():
            ring_b(0)

        @pl.when(i == 4)
        def _():
            ring_a(2)
            relay(2)

        @pl.when(real)
        def _():
            @pl.when(i % 2 == 0)
            def _():
                start_sweep(upper_s, pulled_map, both_s)

            one_pass(both_s)

        return carry

    lax.fori_loop(0, 2 * ITERS, stage, 0)

    @pl.when(real)
    def _():
        window_maps(fbuf, weights_ref, ranks_ref, lower_s, both_s, maps)
        for k in range(1, 4):
            to = (x + k) % 4
            remote(maps.at[to], wall.at[layer, x], sems.at[14], sems.at[15], layer, row_at(z, to)).start()
        pltpu.make_async_copy(maps.at[x], wall.at[layer, x], sems.at[15]).start()

    ring_b(1)
    relay(3)
    ring_a(3)
    other = layer + 1 - 2 * (layer % 2)
    wait_bytes(wall.at[layer], sems.at[15])

    def over(k, index, to):
        return remote(wall.at[index], wall.at[index], over_send.at[k], over_recv.at[k], to, row)

    for k in range(1, 4):
        over(k, layer, (layer + 2 * k) % 8).start()
    over(0, layer, other).start()
    for k in range(1, 4):
        came = (layer + 8 - 2 * k) % 8
        wait_bytes(wall.at[came], over_recv.at[k])
        over(3 + k, came, other).start()
    ring_b(2)
    relay(4)
    ring_b(3)
    for turn in range(5):
        relay_end(turn)
    for step in range(4):
        for group in range(2):
            for copy in ring(step, group):
                copy.wait_send()
    for k in range(1, 4):
        wait_bytes(narrow(0), side_send.at[k - 1])
    wait_bytes(mall.at[pl.ds(0, 7), :, row], sems.at[12])

    @pl.when(real)
    def _():
        wait_bytes(maps.at[pl.ds(0, 3)], sems.at[14])

    wait_bytes(wall.at[other], over_recv.at[0])
    for k in range(1, 4):
        wait_bytes(wall.at[(other + 8 - 2 * k) % 8], over_recv.at[3 + k])
    for k in range(7):
        wait_bytes(wall.at[0], over_send.at[k])


def tile_kernel(maps_ref, model_ref, out_ref):
    for p in range(PROJ):
        model = model_ref[0, p].astype(jnp.float32).reshape(256, 1024).astype(jnp.bfloat16)
        out_ref[0, p] = jnp.dot(
            maps_ref[0, p], model, preferred_element_type=jnp.float32
        ).astype(jnp.bfloat16)


def shards(hidden_stack, model_stack, tenant_weights, ranks, start_basis):
    f32, bf16 = jnp.float32, jnp.bfloat16
    shape = jax.ShapeDtypeStruct
    sem = pltpu.SemaphoreType.DMA
    gram = pltpu.VMEM((8, 16, 384), f32)
    square = pltpu.VMEM((256, 256), f32)
    wall, mall = pl.pallas_call(
        merge_kernel,
        out_shape=[shape((8, PROJ, SERVE_DEV, 256), bf16), shape((8, PROJ, 32, 8, 1024), bf16)],
        in_specs=[ANY, ANY, SM, SM, VM],
        out_specs=[ANY, ANY],
        scratch_shapes=[
            pltpu.VMEM((32, 8, 1024), bf16), pltpu.VMEM((32, 8, 3584), bf16),
            gram, gram, gram, gram, gram, gram,
            square, square, square, pltpu.VMEM((512, 128), f32),
            pltpu.VMEM((4, SERVE_DEV, 256), bf16), sem((16,)),
            sem((2, 2, 4)), sem((2, 2, 4)), sem((3,)), sem((3,)),
            sem((2, 5, 2)), sem((2, 5, 2)), sem((2, 5, 2)), sem((2, 5, 2)),
            sem((7,)), sem((7,)),
        ],
        compiler_params=pltpu.CompilerParams(
            collective_id=0, has_side_effects=True, vmem_limit_bytes=VMEM_BYTES
        ),
    )(hidden_stack, model_stack, tenant_weights, ranks, start_basis)
    return pl.pallas_call(
        tile_kernel,
        grid=(8,),
        out_shape=shape((8, PROJ, SERVE_DEV, 1024), bf16),
        in_specs=[
            pl.BlockSpec((1, PROJ, SERVE_DEV, 256), lambda l: (l, 0, 0, 0)),
            pl.BlockSpec((1, PROJ, 32, 8, 1024), lambda l: (l, 0, 0, 0, 0)),
        ],
        out_specs=pl.BlockSpec((1, PROJ, SERVE_DEV, 1024), lambda l: (l, 0, 0, 0)),
        compiler_params=pltpu.CompilerParams(vmem_limit_bytes=VMEM_BYTES),
    )(wall, mall)


def solution(mesh):
    in_specs = (
        P("layer", None, "row", None),
        P("layer", None, "row", None),
        P(),
        P(),
        P("layer", None, None),
    )
    out_specs = P(None, None, "row", "layer")
    return jax.shard_map(shards, mesh=mesh, in_specs=in_specs, out_specs=out_specs, check_vma=False)
```

```python
import functools
import jax
import jax.numpy as jnp
from jax import lax
from jax.experimental import pallas as pl
from jax.experimental.pallas import tpu as pltpu
from jax.sharding import PartitionSpec as P

ITERS = 3
SERVE_DEV = 64
MOST_RANK = 64
PROJ = 3
SPLIT = 5
HI = lax.Precision.HIGHEST
MESH = pl.DeviceIdType.MESH
VM = pl.BlockSpec(memory_space=pltpu.VMEM)
ANY = pl.BlockSpec(memory_space=pl.ANY)
HBM = pl.BlockSpec(memory_space=pltpu.HBM)
SM = pl.BlockSpec(memory_space=pltpu.SMEM)
VMEM_BYTES = 62 * 1024 * 1024


def dot_hi(a, b, dims):
    return lax.dot_general(a, b, (dims, ((), ())), precision=HI, preferred_element_type=jnp.float32)


def spread_lane(tile, lane):
    return jnp.broadcast_to(tile[:, lane:lane + 1], (8, 128))


def spread_row(tile, row):
    return jnp.broadcast_to(tile[row:row + 1, :], (8, 128))


def total(parts):
    while len(parts) > 1:
        parts = [parts[i] + parts[i + 1] for i in range(0, len(parts), 2)]
    return parts[0]


def factor(matrix, need_upper, need_inverse):
    sub = lax.broadcasted_iota(jnp.int32, (8, 128), 0)
    lane = lax.broadcasted_iota(jnp.int32, (8, 128), 1)
    rowi = lax.broadcasted_iota(jnp.int32, (128, 128), 0)
    coli = lax.broadcasted_iota(jnp.int32, (128, 128), 1)
    own = jnp.where(rowi == coli, matrix, 0.0)
    down = jnp.sum(own, axis=1, keepdims=True)
    across = jnp.sum(own, axis=0, keepdims=True)
    unit_down, unit_across = lax.rsqrt(down), lax.rsqrt(across)
    matrix = matrix * unit_down * unit_across
    rows = [matrix[8 * k:8 * k + 8, :] for k in range(16)]
    inverse = [jnp.where(lane == sub + 8 * k, 1.0, 0.0).astype(jnp.float32) for k in range(16)]
    upper_rows, inverse_rows = [], []
    for k in range(16):
        panel, ipanel = rows[k], inverse[k]
        cols = following if k else [spread_lane(panel, c) for c in range(8)]
        if k < 15:
            ahead = [spread_lane(panel, 8 * k + 8 + c) for c in range(8)]
            raw_next = [spread_lane(rows[k + 1], 8 * k + 8 + c) for c in range(8)]
            coef_next = [spread_lane(rows[k + 1], 8 * k + c) for c in range(8)]
        raw, iraw, diag = panel, ipanel, panel
        for j in range(0, 8, 2):
            first = sub == j
            second = sub == j + 1
            a, b, d = spread_row(cols[j], j), spread_row(cols[j], j + 1), spread_row(cols[j + 1], j + 1)
            recip = 1.0 / (a * d - b * b)
            aa, ab, bb = d * recip, -b * recip, a * recip
            one, two = cols[j], cols[j + 1]
            low = jnp.where(first, -aa, jnp.where(second, -ab, one * aa + two * ab))
            high = jnp.where(first, -ab, jnp.where(second, -bb, one * ab + two * bb))
            ratio = b / a
            diag = jnp.where(first, a, jnp.where(second, d - b * ratio, diag))
            pair = first | second

            def clear(tile):
                p, q = spread_row(tile, j), spread_row(tile, j + 1)
                return p, q, jnp.where(pair, 0.0, tile) - low * p - high * q

            p, q, panel = clear(panel)
            raw = jnp.where(first, p, jnp.where(second, q - ratio * p, raw))
            if need_inverse:
                p, q, ipanel = clear(ipanel)
                iraw = jnp.where(first, p, jnp.where(second, q - ratio * p, iraw))
            for c in range(j + 2, 8):
                cols[c] = clear(cols[c])[2]
            if k < 15:
                ahead = [clear(tile)[2] for tile in ahead]
        root = lax.rsqrt(diag)
        upper_rows.append(raw * root)
        inverse_rows.append(iraw * root)
        prows = [spread_row(panel, c) for c in range(8)]
        irows = [spread_row(ipanel, c) for c in range(8)]
        if k < 15:
            following = [
                raw_next[c] - total([coef_next[j] * spread_row(ahead[c], j) for j in range(8)])
                for c in range(8)
            ]
        for i in range(k + 1, 16):
            coef = [spread_lane(rows[i], 8 * k + c) for c in range(8)]
            rows[i] = rows[i] - total([coef[c] * prows[c] for c in range(8)])
            if need_inverse:
                inverse[i] = inverse[i] - total([coef[c] * irows[c] for c in range(8)])
    out = []
    if need_upper:
        upper = jnp.concatenate(upper_rows, axis=0) * jnp.sqrt(across)
        out.append(jnp.where(coli >= rowi, upper, 0.0))
    if need_inverse:
        out.append(jnp.concatenate(inverse_rows, axis=0) * unit_across)
    return out


def place():
    layer = lax.axis_index("layer")
    row = lax.axis_index("row")
    return layer, row, row // 4, row % 4


def remote(src, dst, send, recv, layer, row):
    return pltpu.make_async_remote_copy(
        src_ref=src, dst_ref=dst, send_sem=send, recv_sem=recv,
        device_id=(layer, row), device_id_type=MESH,
    )


def wait_bytes(ref, sem):
    pltpu.make_async_copy(ref, ref, sem).wait()


def pack_gram(buf, part):
    ranks = buf.shape[0] * buf.shape[1]
    factors = buf[...].astype(jnp.float32).reshape(ranks, buf.shape[2]).astype(jnp.bfloat16)
    gram = lax.dot_general(
        factors, factors, (((1,), (1,)), ((), ())), preferred_element_type=jnp.float32
    )
    part[:, :, 0:128] = gram[0:128, 0:128].reshape(8, 16, 128)
    part[:, :, 128:384] = gram[128:256, :].reshape(8, 16, 256)


def start_reduce(part, slots, send, recv, layer, z, x):
    def one(k, carry):
        to = (z + k) % 8
        remote(part.at[to], slots.at[z], send, recv, layer, to * 4 + x).start()
        return carry

    lax.fori_loop(1, 8, one, 0)
    slots[pl.ds(z, 1)] = part[pl.ds(z, 1)]


def start_share(slots, out, send, recv, send2, recv2, layer, z, x):
    wait_bytes(slots.at[pl.ds(0, 7)], recv)
    wait_bytes(slots.at[pl.ds(0, 7)], send)
    total = slots[0]
    for k in range(1, 8):
        total = total + slots[k]
    out[pl.ds(z, 1)] = total[None]

    def one(k, carry):
        to = (z + k) % 8
        remote(out.at[z], out.at[z], send2, recv2, layer, to * 4 + x).start()
        return carry

    lax.fori_loop(1, 8, one, 0)


def end_share(out, send2, recv2):
    wait_bytes(out.at[pl.ds(0, 7)], recv2)
    wait_bytes(out.at[pl.ds(0, 7)], send2)


def column_scale(ranks_ref, weights_ref, index):
    total = jnp.zeros(index.shape, jnp.float32)
    begin = 0
    for t in range(8):
        end = begin + ranks_ref[t]
        rank = jnp.full(index.shape, ranks_ref[t].astype(jnp.float32))
        factor_t = weights_ref[t] * jnp.sqrt(MOST_RANK / rank)
        total = jnp.where((index >= begin) & (index < end), factor_t, total)
        begin = end
    return total


def lower_factor(gm_ref, weights_ref, ranks_ref, lower_s, upper_s):
    scale_col = column_scale(ranks_ref, weights_ref, lax.broadcasted_iota(jnp.int32, (256, 1), 0))
    scale_row = column_scale(ranks_ref, weights_ref, lax.broadcasted_iota(jnp.int32, (1, 256), 1))
    packed = gm_ref[...].reshape(128, 384)
    first = packed[:, 0:128] * (scale_col[0:128] * scale_row[:, 0:128])
    cross = packed[:, 128:256] * (scale_col[128:256] * scale_row[:, 0:128])
    last = packed[:, 256:384] * (scale_col[128:256] * scale_row[:, 128:256])
    upper_first, inverse_first = factor(first, True, True)
    low = dot_hi(cross, inverse_first, ((1,), (1,)))
    (upper_last,) = factor(last - dot_hi(low, low, ((1,), (1,))), True, False)
    zero = jnp.zeros((128, 128), jnp.float32)
    upper_s[0:128, 0:128] = upper_first
    upper_s[0:128, 128:256] = low.T
    upper_s[128:256, 0:128] = zero
    upper_s[128:256, 128:256] = upper_last
    lower_s[0:128, 0:128] = upper_first.T
    lower_s[0:128, 128:256] = zero
    lower_s[128:256, 0:128] = low
    lower_s[128:256, 128:256] = upper_last.T


def hidden_map(gh_ref, lower_s, pulled_map):
    packed = gh_ref[...].reshape(128, 384)
    hidden = jnp.concatenate(
        [
            jnp.concatenate([packed[:, 0:128], packed[:, 128:256].T], axis=1),
            packed[:, 128:384],
        ],
        axis=0,
    )
    pulled_map[...] = dot_hi(hidden, lower_s[...], ((1,), (0,)))


def start_sweep(upper_s, pulled_map, both_s):
    pushed = dot_hi(pulled_map[...], both_s[0:256, :], ((1,), (0,)))
    both_s[0:256, :] = dot_hi(upper_s[...], pushed, ((1,), (0,)))
    both_s[256:512, :] = pushed


def one_pass(both_s):
    raised = both_s[0:256, :]
    (inverse,) = factor(dot_hi(raised, raised, ((0,), (0,))), False, True)
    both_s[...] = dot_hi(both_s[...], inverse, ((1,), (1,)))


def halves_of(value):
    high = value.astype(jnp.bfloat16)
    return high, (value - high.astype(jnp.float32)).astype(jnp.bfloat16)


def dot_halves(a, b, dims):
    return sum(
        lax.dot_general(a, half, (dims, ((), ())), preferred_element_type=jnp.float32)
        for half in halves_of(b)
    )


def keep_windows(fbuf, windows):
    for j in range(4):
        window = fbuf[:, :, 896 * j:896 * j + 128].astype(jnp.float32).reshape(256, 128)
        windows[j] = window.T[0:SERVE_DEV].astype(jnp.bfloat16)


def window_maps(windows, weights_ref, ranks_ref, lower_s, both_s, maps):
    scale_col = column_scale(ranks_ref, weights_ref, lax.broadcasted_iota(jnp.int32, (256, 1), 0))
    lifted = dot_hi(lower_s[...], both_s[0:256, :], ((1,), (0,)))
    pulled = scale_col * both_s[256:512, :]
    left = dot_halves(windows[...].reshape(4 * SERVE_DEV, 256), lifted, ((1,), (0,)))
    product = dot_halves(left.astype(jnp.bfloat16), pulled, ((1,), (1,)))
    maps[...] = product.astype(jnp.bfloat16).reshape(4, SERVE_DEV, 256)


def merge_kernel(f_ref, m_ref, weights_in, ranks_in, start_ref, wall, mall, weights_ref, ranks_ref,
                 mbuf, fbuf, windows,
                 part_m, part_h, slots_m, slots_h, gm_ref, gh_ref,
                 lower_s, upper_s, pulled_map, both_s, maps, sems,
                 ring_send, ring_recv, side_send, side_recv, wide_send, wide_recv, pass_send, pass_recv,
                 over_send, over_recv, map_recv, load_sems):
    layer, row, z, x = place()
    real = x < PROJ
    loads = [
        pltpu.make_async_copy(weights_in, weights_ref, load_sems.at[0]),
        pltpu.make_async_copy(ranks_in, ranks_ref, load_sems.at[1]),
        pltpu.make_async_copy(start_ref.at[0], both_s.at[pl.ds(0, 256)], load_sems.at[2]),
    ]
    for load in loads:
        load.start()
    barrier = pltpu.get_barrier_semaphore()

    def greet(k, carry):
        pl.semaphore_signal(barrier, inc=1, device_id=(layer, (row + k) % 32), device_id_type=MESH)
        return carry

    lax.fori_loop(1, 32, greet, 0)
    for k in range(1, 8):
        pl.semaphore_signal(barrier, inc=1, device_id=((layer + k) % 8, row), device_id_type=MESH)
    pl.semaphore_wait(barrier, 38)

    def row_at(to_z, to_x):
        return (to_z % 8) * 4 + to_x % 4

    mwide, fwide = mbuf.shape[2], fbuf.shape[2]

    def pieces(src_ref, wide, to):
        column = pl.multiple_of((to // 4) * wide, 128)
        return src_ref.at[0, to % 4, :, pl.ds(column, wide)]

    def scatter(src_ref, buf, wide, base, low, high):
        def send(k, carry):
            to = (row + k) % 32

            @pl.when(to % 4 < PROJ)
            def _():
                remote(
                    pieces(src_ref, wide, to), buf.at[row], sems.at[base], sems.at[base + 1], layer, to
                ).start()

            return carry

        lax.fori_loop(low, high, send, 0)

    def keep(src_ref, buf, wide, base):
        pltpu.make_async_copy(pieces(src_ref, wide, row), buf.at[row], sems.at[base + 1]).start()

    def owned(to):
        return m_ref.at[0, :, :, pl.ds(pl.multiple_of(to * 1024, 128), 1024)]

    def shard(p, c, low=0, wide=1024):
        return mall.at[pl.ds(0, SPLIT), :, (c % 8) * 4 + p, :, pl.ds(low, wide)]

    def thick(c, low=0, count=4):
        return mall.at[pl.ds(SPLIT, 8 - SPLIT), :, pl.ds((c % 8) * 4 + low, count)]

    def halves(step, group, up_c, down_c):
        if group:
            return (thick(up_c), thick(down_c)) if step < 3 else (thick(up_c, 0, 2), thick(down_c, 2, 2))
        if step < 3:
            return shard(x, up_c), shard(x, down_c)
        return shard(x, up_c, 0, 512), shard(x, down_c, 512, 512)

    def ring(step, group):
        up, down = halves(step, group, z + 8 - step, z + step)
        return (
            remote(up, up, ring_send.at[group, 0, step], ring_recv.at[group, 0, step], layer, row_at(z + 1, x)),
            remote(down, down, ring_send.at[group, 1, step], ring_recv.at[group, 1, step],
                   layer, row_at(z + 7, x)),
        )

    def ring_start(step, group):
        for copy in ring(step, group):
            copy.start()

    def ring_got(step, group):
        up, down = halves(step, group, z + 7 - step, z + 1 + step)
        wait_bytes(up, ring_recv.at[group, 0, step])
        wait_bytes(down, ring_recv.at[group, 1, step])

    def columns(turn):
        if turn == 0:
            return (z,)
        if turn == 4:
            return (z + 4,)
        return (z + 8 - turn, z + turn)

    def widen(turn):
        for n, c in enumerate(columns(turn)):
            piece = shard(x, c)
            for way in range(2):
                remote(piece, piece, wide_send.at[way, turn, n], wide_recv.at[way, turn, n],
                       layer, row_at(z, x + 1 + 2 * way)).start()

    before, after, far = (x + 3) % 4, (x + 1) % 4, (x + 2) % 4

    def relay(turn):
        for n, c in enumerate(columns(turn)):
            for way, source in enumerate((before, after)):
                wait_bytes(shard(source, c), wide_recv.at[way, turn, n])
                piece = shard(source, c, 512 * way, 512)
                remote(piece, piece, pass_send.at[way, turn, n], pass_recv.at[way, turn, n],
                       layer, row_at(z, x + 1 + 2 * way)).start()

    def relay_end(turn):
        for n, c in enumerate(columns(turn)):
            for way, source in enumerate((before, after)):
                wait_bytes(shard(x, c), wide_send.at[way, turn, n])
                wait_bytes(shard(source, c, 512 * way, 512), pass_send.at[way, turn, n])
                wait_bytes(shard(far, c, 512 * way, 512), pass_recv.at[way, turn, n])

    def narrow(k):
        return mall.at[pl.ds(SPLIT, 8 - SPLIT), :, row_at(z, x + k)]

    def ring_a(step):
        ring_got(step, 0)
        if step < 3:
            ring_start(step + 1, 0)
        widen(step + 1)

    def ring_b(step):
        ring_got(step, 1)
        if step < 3:
            ring_start(step + 1, 1)

    scatter(m_ref, mbuf, mwide, 0, 1, 32)
    for k in range(1, 8):
        to = (layer + k) % 8
        remote(owned(to), mall.at[layer, :, row], sems.at[12], sems.at[13], to, row).start()
    pltpu.make_async_copy(owned(layer), mall.at[layer, :, row], sems.at[13]).start()
    scatter(f_ref, fbuf, fwide, 2, 1, 11)

    @pl.when(real)
    def _():
        keep(m_ref, mbuf, mwide, 0)
        keep(f_ref, fbuf, fwide, 2)
        wait_bytes(mbuf, sems.at[1])
        pack_gram(mbuf, part_m)
        start_reduce(part_m, slots_m, sems.at[4], sems.at[5], layer, z, x)

    scatter(f_ref, fbuf, fwide, 2, 11, 21)

    @pl.when(real)
    def _():
        start_share(slots_m, gm_ref, sems.at[4], sems.at[5], sems.at[6], sems.at[7], layer, z, x)

    scatter(f_ref, fbuf, fwide, 2, 21, 32)
    wait_bytes(mall.at[:, :, row], sems.at[13])
    for k in range(1, 4):
        remote(narrow(0), narrow(0), side_send.at[k - 1], side_recv.at[k - 1], layer, row_at(z, x + k)).start()
    widen(0)
    ring_start(0, 0)
    for load in loads:
        load.wait()

    @pl.when(real)
    def _():
        end_share(gm_ref, sems.at[6], sems.at[7])
        lower_factor(gm_ref, weights_ref, ranks_ref, lower_s, upper_s)
        wait_bytes(fbuf, sems.at[3])
        wait_bytes(mbuf.at[pl.ds(0, 23)], sems.at[0])
        wait_bytes(fbuf.at[pl.ds(0, 23)], sems.at[2])

    @pl.when(jnp.logical_not(real))
    def _():
        wait_bytes(mbuf.at[pl.ds(0, 24)], sems.at[0])
        wait_bytes(fbuf.at[pl.ds(0, 24)], sems.at[2])

    @pl.when(real)
    def _():
        pack_gram(fbuf, part_h)
        start_reduce(part_h, slots_h, sems.at[8], sems.at[9], layer, z, x)

    relay(0)
    ring_a(0)

    @pl.when(real)
    def _():
        keep_windows(fbuf, windows)
        start_share(slots_h, gh_ref, sems.at[8], sems.at[9], sems.at[10], sems.at[11], layer, z, x)

    for k in range(1, 4):
        wait_bytes(narrow(4 - k), side_recv.at[k - 1])
    ring_start(0, 1)

    @pl.when(real)
    def _():
        end_share(gh_ref, sems.at[10], sems.at[11])
        hidden_map(gh_ref, lower_s, pulled_map)

    def stage(i, carry):
        @pl.when(i == 0)
        def _():
            ring_a(1)

        @pl.when(i == 1)
        def _():
            relay(1)

        @pl.when(i == 2)
        def _():
            ring_a(2)
            ring_b(0)

        @pl.when(i == 3)
        def _():
            relay(2)

        @pl.when(i == 4)
        def _():
            ring_a(3)

        @pl.when(i == 5)
        def _():
            ring_b(1)
            relay(3)

        @pl.when(real)
        def _():
            @pl.when(i % 2 == 0)
            def _():
                start_sweep(upper_s, pulled_map, both_s)

            one_pass(both_s)

        return carry

    lax.fori_loop(0, 2 * ITERS, stage, 0)

    other = layer + 1 - 2 * (layer % 2)

    def over(k, index, to):
        return remote(wall.at[index], wall.at[index], over_send.at[k], over_recv.at[k], to, row)

    def over_part(k, p, to):
        return remote(wall.at[layer, p], wall.at[layer, p], over_send.at[k], over_recv.at[k], to, row)

    @pl.when(real)
    def _():
        window_maps(windows, weights_ref, ranks_ref, lower_s, both_s, maps)
        for k in range(1, 4):
            to = (x + k) % 4
            remote(maps.at[to], wall.at[layer, x], sems.at[14], map_recv.at[4 - k],
                   layer, row_at(z, to)).start()
        pltpu.make_async_copy(maps.at[x], wall.at[layer, x], map_recv.at[0]).start()

    for n in range(4):
        p = (x + n) % 4

        @pl.when(p < PROJ)
        def _():
            wait_bytes(wall.at[layer, p], map_recv.at[n])
            for k in range(1, 4):
                over_part(k, p, (layer + 2 * k) % 8).start()
            over_part(0, p, other).start()

    relay(4)
    for k in range(1, 4):
        came = (layer + 8 - 2 * k) % 8
        wait_bytes(wall.at[came], over_recv.at[k])
        over(3 + k, came, other).start()
    ring_b(2)
    ring_b(3)
    for turn in range(5):
        relay_end(turn)
    for step in range(4):
        for group in range(2):
            for copy in ring(step, group):
                copy.wait_send()
    for k in range(1, 4):
        wait_bytes(narrow(0), side_send.at[k - 1])
    wait_bytes(mall.at[pl.ds(0, 7), :, row], sems.at[12])

    @pl.when(real)
    def _():
        wait_bytes(maps.at[pl.ds(0, 3)], sems.at[14])

    wait_bytes(wall.at[other], over_recv.at[0])
    for k in range(1, 4):
        wait_bytes(wall.at[(other + 8 - 2 * k) % 8], over_recv.at[3 + k])
    for k in range(7):
        wait_bytes(wall.at[0], over_send.at[k])


def tile_kernel(maps_ref, model_ref, out_ref):
    for i in range(maps_ref.shape[0]):
        for p in range(PROJ):
            model = model_ref[i, p].reshape(256, 1024)
            out_ref[i, p] = jnp.dot(
                maps_ref[i, p], model, preferred_element_type=jnp.float32
            ).astype(jnp.bfloat16)


def shards(hidden_stack, model_stack, tenant_weights, ranks, start_basis):
    f32, bf16 = jnp.float32, jnp.bfloat16
    shape = jax.ShapeDtypeStruct
    sem = pltpu.SemaphoreType.DMA
    gram = pltpu.VMEM((8, 16, 384), f32)
    square = pltpu.VMEM((256, 256), f32)
    wall, mall = pl.pallas_call(
        merge_kernel,
        out_shape=[shape((8, PROJ, SERVE_DEV, 256), bf16), shape((8, PROJ, 32, 8, 1024), bf16)],
        in_specs=[HBM] * 5,
        out_specs=[ANY, ANY],
        scratch_shapes=[
            pltpu.SMEM((8,), f32), pltpu.SMEM((8,), jnp.int32),
            pltpu.VMEM((32, 8, 1024), bf16), pltpu.VMEM((32, 8, 3584), bf16),
            pltpu.VMEM((4, SERVE_DEV, 256), bf16),
            gram, gram, gram, gram, gram, gram,
            square, square, square, pltpu.VMEM((512, 128), f32),
            pltpu.VMEM((4, SERVE_DEV, 256), bf16), sem((16,)),
            sem((2, 2, 4)), sem((2, 2, 4)), sem((3,)), sem((3,)),
            sem((2, 5, 2)), sem((2, 5, 2)), sem((2, 5, 2)), sem((2, 5, 2)),
            sem((7,)), sem((7,)), sem((4,)), sem((3,)),
        ],
        compiler_params=pltpu.CompilerParams(
            collective_id=0, has_side_effects=True, vmem_limit_bytes=VMEM_BYTES
        ),
    )(hidden_stack, model_stack, tenant_weights, ranks, start_basis)
    return pl.pallas_call(
        tile_kernel,
        grid=(2,),
        out_shape=shape((8, PROJ, SERVE_DEV, 1024), bf16),
        in_specs=[
            pl.BlockSpec((4, PROJ, SERVE_DEV, 256), lambda l: (l, 0, 0, 0)),
            pl.BlockSpec((4, PROJ, 32, 8, 1024), lambda l: (l, 0, 0, 0, 0)),
        ],
        out_specs=pl.BlockSpec((4, PROJ, SERVE_DEV, 1024), lambda l: (l, 0, 0, 0)),
        compiler_params=pltpu.CompilerParams(vmem_limit_bytes=VMEM_BYTES),
    )(wall, mall)


def solution(mesh):
    in_specs = (
        P("layer", None, "row", None),
        P("layer", None, "row", None),
        P(),
        P(),
        P("layer", None, None),
    )
    out_specs = P(None, None, "row", "layer")
    return jax.shard_map(shards, mesh=mesh, in_specs=in_specs, out_specs=out_specs, check_vma=False)
```

```python
import functools
import jax
import jax.numpy as jnp
from jax import lax
from jax.experimental import pallas as pl
from jax.experimental.pallas import tpu as pltpu
from jax.sharding import PartitionSpec as P

ITERS = 3
SERVE_DEV = 64
MOST_RANK = 64
PROJ = 3
SPLIT = 5
HI = lax.Precision.HIGHEST
MESH = pl.DeviceIdType.MESH
VM = pl.BlockSpec(memory_space=pltpu.VMEM)
ANY = pl.BlockSpec(memory_space=pl.ANY)
HBM = pl.BlockSpec(memory_space=pltpu.HBM)
SM = pl.BlockSpec(memory_space=pltpu.SMEM)
VMEM_BYTES = 62 * 1024 * 1024


def dot_hi(a, b, dims):
    return lax.dot_general(a, b, (dims, ((), ())), precision=HI, preferred_element_type=jnp.float32)


def spread_lane(tile, lane):
    return jnp.broadcast_to(tile[:, lane:lane + 1], (8, 128))


def spread_row(tile, row):
    return jnp.broadcast_to(tile[row:row + 1, :], (8, 128))


def total(parts):
    while len(parts) > 1:
        parts = [parts[i] + parts[i + 1] for i in range(0, len(parts), 2)]
    return parts[0]


def factor(matrix, need_upper, need_inverse):
    sub = lax.broadcasted_iota(jnp.int32, (8, 128), 0)
    lane = lax.broadcasted_iota(jnp.int32, (8, 128), 1)
    rowi = lax.broadcasted_iota(jnp.int32, (128, 128), 0)
    coli = lax.broadcasted_iota(jnp.int32, (128, 128), 1)
    own = jnp.where(rowi == coli, matrix, 0.0)
    down = jnp.sum(own, axis=1, keepdims=True)
    across = jnp.sum(own, axis=0, keepdims=True)
    unit_down, unit_across = lax.rsqrt(down), lax.rsqrt(across)
    matrix = matrix * unit_down * unit_across
    rows = [matrix[8 * k:8 * k + 8, :] for k in range(16)]
    inverse = [jnp.where(lane == sub + 8 * k, 1.0, 0.0).astype(jnp.float32) for k in range(16)]
    upper_rows, inverse_rows = [], []
    for k in range(16):
        panel, ipanel = rows[k], inverse[k]
        cols = following if k else [spread_lane(panel, c) for c in range(8)]
        if k < 15:
            ahead = [spread_lane(panel, 8 * k + 8 + c) for c in range(8)]
            raw_next = [spread_lane(rows[k + 1], 8 * k + 8 + c) for c in range(8)]
            coef_next = [spread_lane(rows[k + 1], 8 * k + c) for c in range(8)]
        raw, iraw, diag = panel, ipanel, panel
        for j in range(0, 8, 2):
            first = sub == j
            second = sub == j + 1
            a, b, d = spread_row(cols[j], j), spread_row(cols[j], j + 1), spread_row(cols[j + 1], j + 1)
            recip = 1.0 / (a * d - b * b)
            aa, ab, bb = d * recip, -b * recip, a * recip
            one, two = cols[j], cols[j + 1]
            low = jnp.where(first, -aa, jnp.where(second, -ab, one * aa + two * ab))
            high = jnp.where(first, -ab, jnp.where(second, -bb, one * ab + two * bb))
            ratio = b / a
            diag = jnp.where(first, a, jnp.where(second, d - b * ratio, diag))
            pair = first | second

            def clear(tile):
                p, q = spread_row(tile, j), spread_row(tile, j + 1)
                return p, q, jnp.where(pair, 0.0, tile) - low * p - high * q

            p, q, panel = clear(panel)
            raw = jnp.where(first, p, jnp.where(second, q - ratio * p, raw))
            if need_inverse:
                p, q, ipanel = clear(ipanel)
                iraw = jnp.where(first, p, jnp.where(second, q - ratio * p, iraw))
            for c in range(j + 2, 8):
                cols[c] = clear(cols[c])[2]
            if k < 15:
                ahead = [clear(tile)[2] for tile in ahead]
        root = lax.rsqrt(diag)
        upper_rows.append(raw * root)
        inverse_rows.append(iraw * root)
        prows = [spread_row(panel, c) for c in range(8)]
        irows = [spread_row(ipanel, c) for c in range(8)]
        if k < 15:
            following = [
                raw_next[c] - total([coef_next[j] * spread_row(ahead[c], j) for j in range(8)])
                for c in range(8)
            ]
        for i in range(k + 1, 16):
            coef = [spread_lane(rows[i], 8 * k + c) for c in range(8)]
            rows[i] = rows[i] - total([coef[c] * prows[c] for c in range(8)])
            if need_inverse:
                inverse[i] = inverse[i] - total([coef[c] * irows[c] for c in range(8)])
    out = []
    if need_upper:
        upper = jnp.concatenate(upper_rows, axis=0) * jnp.sqrt(across)
        out.append(jnp.where(coli >= rowi, upper, 0.0))
    if need_inverse:
        out.append(jnp.concatenate(inverse_rows, axis=0) * unit_across)
    return out


def place():
    layer = lax.axis_index("layer")
    row = lax.axis_index("row")
    return layer, row, row // 4, row % 4


def remote(src, dst, send, recv, layer, row):
    return pltpu.make_async_remote_copy(
        src_ref=src, dst_ref=dst, send_sem=send, recv_sem=recv,
        device_id=(layer, row), device_id_type=MESH,
    )


def wait_bytes(ref, sem):
    pltpu.make_async_copy(ref, ref, sem).wait()


def pack_gram(buf, part):
    ranks = buf.shape[0] * buf.shape[1]
    factors = buf[...].astype(jnp.float32).reshape(ranks, buf.shape[2]).astype(jnp.bfloat16)
    gram = lax.dot_general(
        factors, factors, (((1,), (1,)), ((), ())), preferred_element_type=jnp.float32
    )
    part[:, :, 0:128] = gram[0:128, 0:128].reshape(8, 16, 128)
    part[:, :, 128:384] = gram[128:256, :].reshape(8, 16, 256)


def start_reduce(part, slots, send, recv, layer, z, x):
    def one(k, carry):
        to = (z + k) % 8
        remote(part.at[to], slots.at[z], send, recv, layer, to * 4 + x).start()
        return carry

    lax.fori_loop(1, 8, one, 0)
    slots[pl.ds(z, 1)] = part[pl.ds(z, 1)]


def start_share(slots, out, send, recv, send2, recv2, layer, z, x):
    wait_bytes(slots.at[pl.ds(0, 7)], recv)
    wait_bytes(slots.at[pl.ds(0, 7)], send)
    total = slots[0]
    for k in range(1, 8):
        total = total + slots[k]
    out[pl.ds(z, 1)] = total[None]

    def one(k, carry):
        to = (z + k) % 8
        remote(out.at[z], out.at[z], send2, recv2, layer, to * 4 + x).start()
        return carry

    lax.fori_loop(1, 8, one, 0)


def end_share(out, send2, recv2):
    wait_bytes(out.at[pl.ds(0, 7)], recv2)
    wait_bytes(out.at[pl.ds(0, 7)], send2)


def column_scale(ranks_ref, weights_ref, index):
    total = jnp.zeros(index.shape, jnp.float32)
    begin = 0
    for t in range(8):
        end = begin + ranks_ref[t]
        rank = jnp.full(index.shape, ranks_ref[t].astype(jnp.float32))
        factor_t = weights_ref[t] * jnp.sqrt(MOST_RANK / rank)
        total = jnp.where((index >= begin) & (index < end), factor_t, total)
        begin = end
    return total


def lower_factor(gm_ref, weights_ref, ranks_ref, lower_s, upper_s):
    scale_col = column_scale(ranks_ref, weights_ref, lax.broadcasted_iota(jnp.int32, (256, 1), 0))
    scale_row = column_scale(ranks_ref, weights_ref, lax.broadcasted_iota(jnp.int32, (1, 256), 1))
    packed = gm_ref[...].reshape(128, 384)
    first = packed[:, 0:128] * (scale_col[0:128] * scale_row[:, 0:128])
    cross = packed[:, 128:256] * (scale_col[128:256] * scale_row[:, 0:128])
    last = packed[:, 256:384] * (scale_col[128:256] * scale_row[:, 128:256])
    upper_first, inverse_first = factor(first, True, True)
    low = dot_hi(cross, inverse_first, ((1,), (1,)))
    (upper_last,) = factor(last - dot_hi(low, low, ((1,), (1,))), True, False)
    zero = jnp.zeros((128, 128), jnp.float32)
    upper_s[0:128, 0:128] = upper_first
    upper_s[0:128, 128:256] = low.T
    upper_s[128:256, 0:128] = zero
    upper_s[128:256, 128:256] = upper_last
    lower_s[0:128, 0:128] = upper_first.T
    lower_s[0:128, 128:256] = zero
    lower_s[128:256, 0:128] = low
    lower_s[128:256, 128:256] = upper_last.T


def hidden_map(gh_ref, lower_s, pulled_map):
    packed = gh_ref[...].reshape(128, 384)
    hidden = jnp.concatenate(
        [
            jnp.concatenate([packed[:, 0:128], packed[:, 128:256].T], axis=1),
            packed[:, 128:384],
        ],
        axis=0,
    )
    pulled_map[...] = dot_hi(hidden, lower_s[...], ((1,), (0,)))


def start_sweep(upper_s, pulled_map, both_s):
    pushed = dot_hi(pulled_map[...], both_s[0:256, :], ((1,), (0,)))
    both_s[0:256, :] = dot_hi(upper_s[...], pushed, ((1,), (0,)))
    both_s[256:512, :] = pushed


def one_pass(both_s):
    raised = both_s[0:256, :]
    (inverse,) = factor(dot_hi(raised, raised, ((0,), (0,))), False, True)
    both_s[...] = dot_hi(both_s[...], inverse, ((1,), (1,)))


def halves_of(value):
    high = value.astype(jnp.bfloat16)
    return high, (value - high.astype(jnp.float32)).astype(jnp.bfloat16)


def dot_halves(a, b, dims):
    return sum(
        lax.dot_general(a, half, (dims, ((), ())), preferred_element_type=jnp.float32)
        for half in halves_of(b)
    )


def keep_windows(fbuf, windows):
    for j in range(4):
        window = fbuf[:, :, 896 * j:896 * j + 128].astype(jnp.float32).reshape(256, 128)
        windows[j] = window.T[0:SERVE_DEV].astype(jnp.bfloat16)


def window_maps(windows, weights_ref, ranks_ref, lower_s, both_s, maps):
    scale_col = column_scale(ranks_ref, weights_ref, lax.broadcasted_iota(jnp.int32, (256, 1), 0))
    lifted = dot_hi(lower_s[...], both_s[0:256, :], ((1,), (0,)))
    pulled = scale_col * both_s[256:512, :]
    left = dot_halves(windows[...].reshape(4 * SERVE_DEV, 256), lifted, ((1,), (0,)))
    product = dot_halves(left.astype(jnp.bfloat16), pulled, ((1,), (1,)))
    maps[...] = product.astype(jnp.bfloat16).reshape(4, SERVE_DEV, 256)


def merge_kernel(f_ref, m_ref, weights_in, ranks_in, start_ref, wall, mall, weights_ref, ranks_ref,
                 mbuf, fbuf, windows,
                 part_m, part_h, slots_m, slots_h, gm_ref, gh_ref,
                 lower_s, upper_s, pulled_map, both_s, maps, sems,
                 ring_send, ring_recv, side_send, side_recv, wide_send, wide_recv, pass_send, pass_recv,
                 over_send, over_recv, map_recv, load_sems):
    layer, row, z, x = place()
    real = x < PROJ
    loads = [
        pltpu.make_async_copy(weights_in, weights_ref, load_sems.at[0]),
        pltpu.make_async_copy(ranks_in, ranks_ref, load_sems.at[1]),
        pltpu.make_async_copy(start_ref.at[0], both_s.at[pl.ds(0, 256)], load_sems.at[2]),
    ]
    for load in loads:
        load.start()
    barrier = pltpu.get_barrier_semaphore()

    def greet(k, carry):
        pl.semaphore_signal(barrier, inc=1, device_id=(layer, (row + k) % 32), device_id_type=MESH)
        return carry

    lax.fori_loop(1, 32, greet, 0)
    for k in range(1, 8):
        pl.semaphore_signal(barrier, inc=1, device_id=((layer + k) % 8, row), device_id_type=MESH)
    pl.semaphore_wait(barrier, 38)

    def row_at(to_z, to_x):
        return (to_z % 8) * 4 + to_x % 4

    mwide, fwide = mbuf.shape[2], fbuf.shape[2]

    def pieces(src_ref, wide, to):
        column = pl.multiple_of((to // 4) * wide, 128)
        return src_ref.at[0, to % 4, :, pl.ds(column, wide)]

    def scatter(src_ref, buf, wide, base, low, high):
        def send(k, carry):
            to = (row + k) % 32

            @pl.when(to % 4 < PROJ)
            def _():
                remote(
                    pieces(src_ref, wide, to), buf.at[row], sems.at[base], sems.at[base + 1], layer, to
                ).start()

            return carry

        lax.fori_loop(low, high, send, 0)

    def keep(src_ref, buf, wide, base):
        pltpu.make_async_copy(pieces(src_ref, wide, row), buf.at[row], sems.at[base + 1]).start()

    def owned(to):
        return m_ref.at[0, :, :, pl.ds(pl.multiple_of(to * 1024, 128), 1024)]

    def shard(p, c, low=0, wide=1024):
        return mall.at[pl.ds(0, SPLIT), :, (c % 8) * 4 + p, :, pl.ds(low, wide)]

    def thick(c, low=0, count=4):
        return mall.at[pl.ds(SPLIT, 8 - SPLIT), :, pl.ds((c % 8) * 4 + low, count)]

    def halves(step, group, up_c, down_c):
        if group:
            return (thick(up_c), thick(down_c)) if step < 3 else (thick(up_c, 0, 2), thick(down_c, 2, 2))
        if step < 3:
            return shard(x, up_c), shard(x, down_c)
        return shard(x, up_c, 0, 512), shard(x, down_c, 512, 512)

    def ring(step, group):
        up, down = halves(step, group, z + 8 - step, z + step)
        return (
            remote(up, up, ring_send.at[group, 0, step], ring_recv.at[group, 0, step], layer, row_at(z + 1, x)),
            remote(down, down, ring_send.at[group, 1, step], ring_recv.at[group, 1, step],
                   layer, row_at(z + 7, x)),
        )

    def ring_start(step, group):
        for copy in ring(step, group):
            copy.start()

    def ring_got(step, group):
        up, down = halves(step, group, z + 7 - step, z + 1 + step)
        wait_bytes(up, ring_recv.at[group, 0, step])
        wait_bytes(down, ring_recv.at[group, 1, step])

    def columns(turn):
        if turn == 0:
            return (z,)
        if turn == 4:
            return (z + 4,)
        return (z + 8 - turn, z + turn)

    def widen(turn):
        for n, c in enumerate(columns(turn)):
            piece = shard(x, c)
            for way in range(2):
                remote(piece, piece, wide_send.at[way, turn, n], wide_recv.at[way, turn, n],
                       layer, row_at(z, x + 1 + 2 * way)).start()

    before, after, far = (x + 3) % 4, (x + 1) % 4, (x + 2) % 4

    def relay(turn):
        for n, c in enumerate(columns(turn)):
            for way, source in enumerate((before, after)):
                wait_bytes(shard(source, c), wide_recv.at[way, turn, n])
                piece = shard(source, c, 512 * way, 512)
                remote(piece, piece, pass_send.at[way, turn, n], pass_recv.at[way, turn, n],
                       layer, row_at(z, x + 1 + 2 * way)).start()

    def relay_end(turn):
        for n, c in enumerate(columns(turn)):
            for way, source in enumerate((before, after)):
                wait_bytes(shard(x, c), wide_send.at[way, turn, n])
                wait_bytes(shard(source, c, 512 * way, 512), pass_send.at[way, turn, n])
                wait_bytes(shard(far, c, 512 * way, 512), pass_recv.at[way, turn, n])

    def narrow(k):
        return mall.at[pl.ds(SPLIT, 8 - SPLIT), :, row_at(z, x + k)]

    def ring_a(step):
        ring_got(step, 0)
        if step < 3:
            ring_start(step + 1, 0)
        widen(step + 1)

    def ring_b(step):
        ring_got(step, 1)
        if step < 3:
            ring_start(step + 1, 1)

    scatter(m_ref, mbuf, mwide, 0, 1, 32)
    for k in range(1, 8):
        to = (layer + k) % 8
        remote(owned(to), mall.at[layer, :, row], sems.at[12], sems.at[13], to, row).start()
    pltpu.make_async_copy(owned(layer), mall.at[layer, :, row], sems.at[13]).start()
    scatter(f_ref, fbuf, fwide, 2, 1, 11)

    @pl.when(real)
    def _():
        keep(m_ref, mbuf, mwide, 0)
        keep(f_ref, fbuf, fwide, 2)
        wait_bytes(mbuf, sems.at[1])
        pack_gram(mbuf, part_m)
        start_reduce(part_m, slots_m, sems.at[4], sems.at[5], layer, z, x)

    scatter(f_ref, fbuf, fwide, 2, 11, 21)

    @pl.when(real)
    def _():
        start_share(slots_m, gm_ref, sems.at[4], sems.at[5], sems.at[6], sems.at[7], layer, z, x)

    scatter(f_ref, fbuf, fwide, 2, 21, 32)
    wait_bytes(mall.at[:, :, row], sems.at[13])
    for k in range(1, 4):
        remote(narrow(0), narrow(0), side_send.at[k - 1], side_recv.at[k - 1], layer, row_at(z, x + k)).start()
    widen(0)
    ring_start(0, 0)
    for load in loads:
        load.wait()

    @pl.when(real)
    def _():
        end_share(gm_ref, sems.at[6], sems.at[7])
        lower_factor(gm_ref, weights_ref, ranks_ref, lower_s, upper_s)
        wait_bytes(fbuf, sems.at[3])
        wait_bytes(mbuf.at[pl.ds(0, 23)], sems.at[0])
        wait_bytes(fbuf.at[pl.ds(0, 23)], sems.at[2])

    @pl.when(jnp.logical_not(real))
    def _():
        wait_bytes(mbuf.at[pl.ds(0, 24)], sems.at[0])
        wait_bytes(fbuf.at[pl.ds(0, 24)], sems.at[2])

    @pl.when(real)
    def _():
        pack_gram(fbuf, part_h)
        start_reduce(part_h, slots_h, sems.at[8], sems.at[9], layer, z, x)

    relay(0)
    ring_a(0)

    @pl.when(real)
    def _():
        keep_windows(fbuf, windows)
        start_share(slots_h, gh_ref, sems.at[8], sems.at[9], sems.at[10], sems.at[11], layer, z, x)

    for k in range(1, 4):
        wait_bytes(narrow(4 - k), side_recv.at[k - 1])
    ring_start(0, 1)

    @pl.when(real)
    def _():
        end_share(gh_ref, sems.at[10], sems.at[11])
        hidden_map(gh_ref, lower_s, pulled_map)

    def stage(i, carry):
        @pl.when(i == 0)
        def _():
            ring_a(1)

        @pl.when(i == 1)
        def _():
            relay(1)

        @pl.when(i == 2)
        def _():
            ring_a(2)
            ring_b(0)

        @pl.when(i == 3)
        def _():
            relay(2)

        @pl.when(i == 4)
        def _():
            ring_a(3)

        @pl.when(i == 5)
        def _():
            ring_b(1)
            relay(3)

        @pl.when(real)
        def _():
            @pl.when(i % 2 == 0)
            def _():
                start_sweep(upper_s, pulled_map, both_s)

            one_pass(both_s)

        return carry

    lax.fori_loop(0, 2 * ITERS, stage, 0)

    other = layer + 1 - 2 * (layer % 2)

    def over(k, index, to):
        return remote(wall.at[index], wall.at[index], over_send.at[k], over_recv.at[k], to, row)

    def over_part(k, p, to):
        return remote(wall.at[layer, p], wall.at[layer, p], over_send.at[k], over_recv.at[k], to, row)

    @pl.when(real)
    def _():
        window_maps(windows, weights_ref, ranks_ref, lower_s, both_s, maps)
        for k in range(1, 4):
            to = (x + k) % 4
            remote(maps.at[to], wall.at[layer, x], sems.at[14], map_recv.at[4 - k],
                   layer, row_at(z, to)).start()
        pltpu.make_async_copy(maps.at[x], wall.at[layer, x], map_recv.at[0]).start()

    for n in range(4):
        p = (x + n) % 4

        @pl.when(p < PROJ)
        def _():
            wait_bytes(wall.at[layer, p], map_recv.at[n])
            for k in range(1, 4):
                over_part(k, p, (layer + 2 * k) % 8).start()
            over_part(0, p, other).start()

    relay(4)
    ring_b(2)
    for k in range(1, 4):
        came = (layer + 8 - 2 * k) % 8
        wait_bytes(wall.at[came], over_recv.at[k])
        over(3 + k, came, other).start()
    ring_b(3)
    for turn in range(5):
        relay_end(turn)
    for step in range(4):
        for group in range(2):
            for copy in ring(step, group):
                copy.wait_send()
    for k in range(1, 4):
        wait_bytes(narrow(0), side_send.at[k - 1])
    wait_bytes(mall.at[pl.ds(0, 7), :, row], sems.at[12])

    @pl.when(real)
    def _():
        wait_bytes(maps.at[pl.ds(0, 3)], sems.at[14])

    wait_bytes(wall.at[other], over_recv.at[0])
    for k in range(1, 4):
        wait_bytes(wall.at[(other + 8 - 2 * k) % 8], over_recv.at[3 + k])
    for k in range(7):
        wait_bytes(wall.at[0], over_send.at[k])


def tile_kernel(maps_ref, model_ref, out_ref):
    for i in range(maps_ref.shape[0]):
        for p in range(PROJ):
            model = model_ref[i, p].reshape(256, 1024)
            out_ref[i, p] = jnp.dot(
                maps_ref[i, p], model, preferred_element_type=jnp.float32
            ).astype(jnp.bfloat16)


def shards(hidden_stack, model_stack, tenant_weights, ranks, start_basis):
    f32, bf16 = jnp.float32, jnp.bfloat16
    shape = jax.ShapeDtypeStruct
    sem = pltpu.SemaphoreType.DMA
    gram = pltpu.VMEM((8, 16, 384), f32)
    square = pltpu.VMEM((256, 256), f32)
    wall, mall = pl.pallas_call(
        merge_kernel,
        out_shape=[shape((8, PROJ, SERVE_DEV, 256), bf16), shape((8, PROJ, 32, 8, 1024), bf16)],
        in_specs=[HBM] * 5,
        out_specs=[ANY, ANY],
        scratch_shapes=[
            pltpu.SMEM((8,), f32), pltpu.SMEM((8,), jnp.int32),
            pltpu.VMEM((32, 8, 1024), bf16), pltpu.VMEM((32, 8, 3584), bf16),
            pltpu.VMEM((4, SERVE_DEV, 256), bf16),
            gram, gram, gram, gram, gram, gram,
            square, square, square, pltpu.VMEM((512, 128), f32),
            pltpu.VMEM((4, SERVE_DEV, 256), bf16), sem((16,)),
            sem((2, 2, 4)), sem((2, 2, 4)), sem((3,)), sem((3,)),
            sem((2, 5, 2)), sem((2, 5, 2)), sem((2, 5, 2)), sem((2, 5, 2)),
            sem((7,)), sem((7,)), sem((4,)), sem((3,)),
        ],
        compiler_params=pltpu.CompilerParams(
            collective_id=0, has_side_effects=True, vmem_limit_bytes=VMEM_BYTES
        ),
    )(hidden_stack, model_stack, tenant_weights, ranks, start_basis)
    return pl.pallas_call(
        tile_kernel,
        grid=(2,),
        out_shape=shape((8, PROJ, SERVE_DEV, 1024), bf16),
        in_specs=[
            pl.BlockSpec((4, PROJ, SERVE_DEV, 256), lambda l: (l, 0, 0, 0)),
            pl.BlockSpec((4, PROJ, 32, 8, 1024), lambda l: (l, 0, 0, 0, 0)),
        ],
        out_specs=pl.BlockSpec((4, PROJ, SERVE_DEV, 1024), lambda l: (l, 0, 0, 0)),
        compiler_params=pltpu.CompilerParams(vmem_limit_bytes=VMEM_BYTES),
    )(wall, mall)


def solution(mesh):
    in_specs = (
        P("layer", None, "row", None),
        P("layer", None, "row", None),
        P(),
        P(),
        P("layer", None, None),
    )
    out_specs = P(None, None, "row", "layer")
    return jax.shard_map(shards, mesh=mesh, in_specs=in_specs, out_specs=out_specs, check_vma=False)
```
